256 devices in a mesh: dp: 32 (over y, z_hi, x), seq: 8 (over z_lo, core).
Axes of the slice: x: 4, y: 4, z: 8 (z_hi: 2, z_lo: 4; z = z_hi * 4 + z_lo), core: 2. Of those that a mesh axis runs over, the one named last changes fastest.
Arguments:
- prompt_hidden: bfloat16 [32, 2048, 5120], P('dp', 'seq'), may hold values from -6 to 6
- key_value_weight: bfloat16 [5120, 2048], P(('dp', 'seq')), may hold values from -0.078125 to 0.078125
- key_norm_gain: float32 [1024], replicated, may hold values from 0.25 to 1.75
- page_table: int32 [32, 16], replicated, may hold values from 0 to 15, each once within a row
- lengths: int32 [32], replicated, may hold values from 512 to 2048, as said below
- source_replica: int32 [32], replicated, may hold values from 0 to 31, as said below
- decode_hidden: bfloat16 [3, 512, 5120], P(None, 'dp'), may hold values from -6 to 6
- queries: bfloat16 [3, 512, 5120], P(None, 'dp', 'seq'), may hold values from -1 to 1
Outputs:
- attended: bfloat16 [3, 512, 5120], P(None, 'dp', 'seq')
- forked_cache: float32 [32, 2, 2048, 1024], P('dp', None, None, 'seq')
The draws below stay inside these ranges and needn't reach their ends.
Inputs may be any that keep to these rules, and one draw needn't show every extreme that they name: `lengths`: some prompt has exactly 2048 tokens and some exactly 512. source_replica[r] is r XOR one nonzero number that is the same for all replicas.
All inputs are finite; a program needn't handle non-finite values.
Results may differ from the reference program's by a relative error of at most 0.0059.
Values may be sent and summed in bfloat16 or wider, within the bound.
A program may use at most 128 MiB of HBM per device.

```python
import math
import jax
import jax.numpy as jnp
from jax import lax

MODEL_WIDTH = 5120
HQ = 40
KEY_VALUE_HEADS = 8
HEAD_SIZE = 128
PAGE_TOKENS = 128
DECODE_STEPS = 3
SAMP = 8
QUERY_PER_KV = 5
PAGES = 16
LMAX = 2048
PROMPTS = 32
TOTAL_SAMPLES = 512
N_DP = 32


def draw_lengths(key, part):
    key = jax.random.fold_in(key, 11)
    first, second = jax.random.split(key)
    values = jax.random.randint(first, (PROMPTS,), LMAX // 4, LMAX + 1)
    order = jax.random.permutation(second, PROMPTS)
    values = values.at[order[0]].set(LMAX)
    values = values.at[order[1]].set(LMAX // 4)
    return values.astype(jnp.int32)


def draw_source_replica(key, part):
    key = jax.random.fold_in(key, 23)
    partner = jax.random.randint(key, (), 1, N_DP)
    return jnp.bitwise_xor(jnp.arange(N_DP, dtype=jnp.int32), partner).astype(jnp.int32)


def steps_of(key, dims, pieces, low, high):
    factor_of = 1.0
    for position, parts in pieces:
        steps = jax.random.uniform(jax.random.fold_in(jax.random.fold_in(key, 6), position), (parts,), jnp.float32, low / len(pieces), high / len(pieces))
        factor_of = factor_of * jnp.repeat(jnp.exp(steps), dims[position] // parts).reshape((-1,) + (1,) * (len(dims) - 1 - position))
    return factor_of


def normal_values(rng, extent, deviation, reach, pieces=(), kind=jnp.bfloat16):
    factor_of = steps_of(rng, extent, pieces, -0.22, 0.18) if pieces else 1.0
    entries = jax.random.normal(rng, extent, jnp.float32) * deviation * factor_of
    return jnp.minimum(jnp.maximum(entries, -reach), reach).astype(kind)


def setup_inputs(seed: int = 0) -> dict:
    seeds = jax.random.split(jax.random.key(seed), 9)
    return {
        "prompt_hidden": normal_values(seeds[0], (PROMPTS, LMAX, MODEL_WIDTH), 1.0, 6.0, ((0, 32), (1, 8))),
        "key_value_weight": normal_values(seeds[1], (MODEL_WIDTH, 2 * KEY_VALUE_HEADS * HEAD_SIZE), MODEL_WIDTH ** -0.5, 0.078125, ((0, 256),)),
        "key_norm_gain": jnp.clip(1.0 + 0.15 * jax.random.normal(seeds[2], (KEY_VALUE_HEADS * HEAD_SIZE,), jnp.float32), 0.25, 1.75),
        "page_table": jax.vmap(lambda own: jax.random.permutation(own, PAGES))(jax.random.split(seeds[3], PROMPTS)).reshape((PROMPTS, PAGES)).astype(jnp.int32),
        "lengths": draw_lengths(jax.random.fold_in(seeds[8], 71), 0),
        "source_replica": draw_source_replica(jax.random.fold_in(seeds[8], 71), 0),
        "decode_hidden": normal_values(seeds[6], (DECODE_STEPS, TOTAL_SAMPLES, MODEL_WIDTH), 1.0, 6.0, ((1, 32),)),
        "queries": jnp.clip(jax.random.uniform(seeds[7], (DECODE_STEPS, TOTAL_SAMPLES, HQ * HEAD_SIZE), jnp.float32, -1.0, 1.0) * steps_of(seeds[7], (DECODE_STEPS, TOTAL_SAMPLES, HQ * HEAD_SIZE), ((1, 32), (2, 8)), -0.4, 0.0), -1.0, 1.0).astype(jnp.bfloat16),
    }


def page_positions(table):
    return (table[:, None] * PAGE_TOKENS + jnp.arange(PAGE_TOKENS, dtype=jnp.int32)[None, :]).reshape(-1)

def root_mean_keys(raw_keys, norm_gain):
    return raw_keys * lax.rsqrt(lax.optimization_barrier(jnp.mean(raw_keys * raw_keys, axis=-1, keepdims=True)) + 1e-06) * norm_gain

def rotate(head_split, places):
    half = head_split.shape[-1] // 2
    freq = 500000.0 ** (-jnp.arange(half, dtype=jnp.float32) * 2.0 / head_split.shape[-1])
    angle = places.astype(jnp.float32)[..., None, None] * freq
    cosine = jnp.cos(angle)
    sine = jnp.sin(angle)
    first = head_split[..., :half]
    second = head_split[..., half:]
    return jnp.concatenate([first * cosine - second * sine, second * cosine + first * sine], axis=-1)

def prepare(projected_rows, norm_gain, places, length):
    key_width = KEY_VALUE_HEADS * HEAD_SIZE
    key_rows = root_mean_keys(projected_rows[:, :key_width], norm_gain).reshape(-1, KEY_VALUE_HEADS, HEAD_SIZE)
    key_rows = rotate(key_rows, places).reshape(-1, key_width)
    values = projected_rows[:, key_width:]
    live = (places < length)[None, :, None]
    return jnp.where(live, jnp.stack([key_rows, values]), jnp.float32(0.0))

def quantize(cache_fields):
    token_count = cache_fields.shape[1]
    paged_cache = cache_fields.reshape(2, token_count // PAGE_TOKENS, PAGE_TOKENS, KEY_VALUE_HEADS, HEAD_SIZE)
    largest = lax.optimization_barrier(jnp.max(jnp.abs(paged_cache), axis=(2, 4)))
    inverse_scale = ((largest + 1e-06) / 448.0).astype(jnp.bfloat16)
    stored_pages = (paged_cache / inverse_scale[:, :, None, :, None].astype(jnp.float32)).astype(jnp.bfloat16)
    return (stored_pages.reshape(2, token_count, KEY_VALUE_HEADS * HEAD_SIZE), inverse_scale)

def expand(pool, inverse_scale):
    token_count = pool.shape[1]
    head_split = inverse_scale.shape[2]
    paged_cache = pool.reshape(2, token_count // PAGE_TOKENS, PAGE_TOKENS, head_split, HEAD_SIZE).astype(jnp.float32)
    return (paged_cache * inverse_scale[:, :, None, :, None].astype(jnp.float32)).reshape(2, token_count, head_split * HEAD_SIZE)

def attend(head_split, pool, inverse_scale, places, length, fresh_key_rows, fresh_value_rows):
    steps = head_split.shape[0]
    groups = head_split.shape[2]
    key_rows = pool[0].reshape(-1, groups, HEAD_SIZE).astype(jnp.float32)
    values = pool[1].reshape(-1, groups, HEAD_SIZE).astype(jnp.float32)
    factor = 1.0 / math.sqrt(HEAD_SIZE)
    key_scale = jnp.repeat(inverse_scale[0].astype(jnp.float32), PAGE_TOKENS, axis=0).T
    value_scale = jnp.repeat(inverse_scale[1].astype(jnp.float32), PAGE_TOKENS, axis=0).T
    query = head_split.astype(jnp.float32)
    raw = jnp.einsum('sijgd,tjd->sijgt', query, key_rows)
    cached = jnp.where(places < length, jnp.exp(raw * key_scale[None, None, :, None, :] * factor), jnp.float32(0.0))
    fresh_raw = jnp.einsum('sijgd,uijd->sijgu', query, fresh_key_rows.astype(jnp.float32))
    visible = jnp.arange(steps)[:, None] >= jnp.arange(steps)[None, :]
    fresh = jnp.where(visible[:, None, None, None, :], jnp.exp(fresh_raw * factor), jnp.float32(0.0))
    total = lax.optimization_barrier(jnp.sum(cached, axis=-1)) + lax.optimization_barrier(jnp.sum(fresh, axis=-1))
    cached_weight = (cached / total[..., None] * value_scale[None, None, :, None, :]).astype(jnp.bfloat16)
    fresh_weight = (fresh / total[..., None]).astype(jnp.bfloat16)
    result = jnp.einsum('sijgt,tjd->sijgd', cached_weight.astype(jnp.float32), values)
    return result + jnp.einsum('sijgu,uijd->sijgd', fresh_weight.astype(jnp.float32), fresh_value_rows.astype(jnp.float32))

def reference(prompt_hidden, key_value_weight, key_norm_gain, page_table, lengths, source_replica, decode_hidden, queries):
    positions = jax.vmap(page_positions)(page_table)

    def prefill(item):
        hidden_rows, places, length = item
        projected_rows = jnp.dot(hidden_rows, key_value_weight, preferred_element_type=jnp.float32)
        return quantize(prepare(projected_rows, key_norm_gain, places, length))
    stored_pages, scales = lax.map(prefill, (prompt_hidden, positions, lengths))
    decode_portion = jnp.dot(decode_hidden.reshape(DECODE_STEPS * TOTAL_SAMPLES, MODEL_WIDTH), key_value_weight, preferred_element_type=jnp.float32)
    decode_portion = decode_portion.reshape(DECODE_STEPS, TOTAL_SAMPLES, 2 * KEY_VALUE_HEADS * HEAD_SIZE)
    sample_index = jnp.arange(TOTAL_SAMPLES, dtype=jnp.int32)
    owner = sample_index // (2 * SAMP)
    prompt_of = jnp.where(sample_index // SAMP % 2 == 0, owner, source_replica[owner])
    new_places = lengths[prompt_of][None, :] + jnp.arange(DECODE_STEPS, dtype=jnp.int32)[:, None]
    fresh_key_rows = root_mean_keys(decode_portion[..., :KEY_VALUE_HEADS * HEAD_SIZE], key_norm_gain).reshape(DECODE_STEPS, TOTAL_SAMPLES, KEY_VALUE_HEADS, HEAD_SIZE)
    fresh_key_rows = rotate(fresh_key_rows, new_places).astype(jnp.bfloat16)
    fresh_value_rows = decode_portion[..., KEY_VALUE_HEADS * HEAD_SIZE:].reshape(DECODE_STEPS, TOTAL_SAMPLES, KEY_VALUE_HEADS, HEAD_SIZE).astype(jnp.bfloat16)
    head_split = queries.reshape(DECODE_STEPS, TOTAL_SAMPLES, KEY_VALUE_HEADS, QUERY_PER_KV, HEAD_SIZE)

    def serve(replica):
        start = replica * 2 * SAMP
        local_heads = lax.dynamic_slice_in_dim(head_split, start, 2 * SAMP, 1)
        local_keys = lax.dynamic_slice_in_dim(fresh_key_rows, start, 2 * SAMP, 1)
        local_values = lax.dynamic_slice_in_dim(fresh_value_rows, start, 2 * SAMP, 1)
        partner = source_replica[replica]
        near = attend(local_heads[:, :SAMP], stored_pages[replica], scales[replica], positions[replica], lengths[replica], local_keys[:, :SAMP], local_values[:, :SAMP])
        far = attend(local_heads[:, SAMP:], stored_pages[partner], scales[partner], positions[partner], lengths[partner], local_keys[:, SAMP:], local_values[:, SAMP:])
        fork = expand(stored_pages[partner], scales[partner])
        return (jnp.concatenate([near, far], axis=1).astype(jnp.bfloat16), fork)
    served, forked_cache = lax.map(serve, jnp.arange(N_DP, dtype=jnp.int32))
    served = jnp.transpose(served, (1, 0, 2, 3, 4, 5))
    return (served.reshape(DECODE_STEPS, TOTAL_SAMPLES, HQ * HEAD_SIZE), forked_cache)
```

```python
import math

import jax
import jax.numpy as jnp
from jax import lax
from jax.experimental import pallas as pl
from jax.experimental.pallas import tpu as pltpu
from jax.sharding import PartitionSpec as P

HEADS = 8
HEAD = 128
PAGE = 128
GROUP = 5
MESH = pl.DeviceIdType.MESH
F32 = jnp.float32
BF16 = jnp.bfloat16

WIDTH = 5120
SHARD = 20
PADDED = 32
PAIR_ROWS = 80
BLOCK = 160
TOKENS = 256
CHIP_TOKENS = 512
FRESH = 48
ROWS = CHIP_TOKENS + FRESH
SLAB = CHIP_TOKENS + 16
LANES = 128


def gather_project(
    w_ref,
    prompt_ref,
    decode_ref,
    cos_ref,
    sin_ref,
    live_ref,
    gain_ref,
    pool_ref,
    fresh_ref,
    raw,
    acts,
    weights,
    acc,
    stage,
    squares,
    send_sem,
    recv_sem,
    local_sem,
):
    dp = lax.axis_index("dp")
    seq = lax.axis_index("seq")
    core = lax.rem(seq, 2)
    z_lo = seq // 2
    x = lax.rem(dp, 4)
    z_hi = lax.rem(dp // 4, 2)
    y = dp // 8
    z = z_hi * 4 + z_lo
    pair = z // 2
    odd = lax.rem(z, 2)

    def at(yy, zz, xx, cc):
        return (yy * 8 + (zz // 4) * 4 + xx, lax.rem(zz, 4) * 2 + cc)

    def turn(index, by, size):
        return lax.rem(index + (by + size), size)

    sibling = at(y, z, x, 1 - core)
    inter_z = turn(z, 2 * odd - 1, 8)
    intra_z = z + 1 - 2 * odd
    inter = at(y, inter_z, x, core)
    intra = at(y, intra_z, x, core)
    intra_other = at(y, intra_z, x, 1 - core)
    rights = {"x": at(y, z, turn(x, 1, 4), core), "y": at(turn(y, 1, 4), z, x, core)}
    lefts = {"x": at(y, z, turn(x, -1, 4), core), "y": at(turn(y, -1, 4), z, x, core)}
    far_chips = [jnp.bitwise_xor(z_lo, d) for d in (1, 2, 3)]
    columns = [(dp, chip * 2 + core) for chip in far_chips]

    peers = [
        sibling,
        inter,
        intra,
        intra_other,
        rights["x"],
        lefts["x"],
        rights["y"],
        lefts["y"],
        columns[1],
        columns[2],
    ]
    barrier = pltpu.get_barrier_semaphore()
    for peer in peers:
        pl.semaphore_signal(barrier, inc=1, device_id=peer, device_id_type=MESH)
    pl.semaphore_wait(barrier, len(peers))

    number = [0]
    copies = {}

    def send(key, src, dst, device):
        k = number[0]
        number[0] += 1
        copy = pltpu.make_async_remote_copy(
            src_ref=src,
            dst_ref=dst,
            send_sem=send_sem.at[k],
            recv_sem=recv_sem.at[k],
            device_id=device,
            device_id_type=MESH,
        )
        copy.start()
        copies[key] = copy

    def arrived(*keys):
        for key in keys:
            copies[key].wait_recv()

    slot = odd * 2 + core
    mine = w_ref.at[core]
    other = w_ref.at[1 - core]
    send("w_intra", mine, raw.at[slot], intra)
    send("w_other", other, raw.at[slot], intra_other)
    send("w_sibling", other, raw.at[slot], sibling)

    here = pl.ds(pl.multiple_of(core * TOKENS, TOKENS), TOKENS)
    send("acts", prompt_ref, acts.at[here], sibling)
    own_acts = pltpu.make_async_copy(prompt_ref, acts.at[here], local_sem.at[0])
    own_acts.start()
    own_decode = pltpu.make_async_copy(
        decode_ref, acts.at[pl.ds(CHIP_TOKENS, FRESH)], local_sem.at[1]
    )
    own_decode.start()

    raw[slot] = w_ref[core]
    arrived("w_intra", "w_other", "w_sibling")
    row = lax.broadcasted_iota(jnp.int32, (PAIR_ROWS, 4 * PADDED), 0)
    col = lax.broadcasted_iota(jnp.int32, (PAIR_ROWS, 4 * PADDED), 1)
    inside = jnp.bitwise_and(col, PADDED - 1)
    source = jnp.right_shift(col, 5)
    pick = jnp.where((row == source * SHARD + inside) & (inside < SHARD), 1.0, 0.0).astype(BF16)
    rows = jnp.dot(
        pick, raw[...].reshape(4 * PADDED, 8 * LANES), preferred_element_type=F32
    ).astype(BF16)

    outer = (y, x)
    inner = (x, y)
    inner_axis = ("x", "y")
    outer_axis = ("y", "x")
    for g in range(2):
        for p in range(2):
            for t in range(2):
                tile = g * 4 + p * 2 + t
                weights[g, p, outer[p], pair, inner[p], pl.ds(t * PAIR_ROWS, PAIR_ROWS)] = rows[
                    :, tile * LANES : (tile + 1) * LANES
                ]

    sign = 2 * odd - 1
    blocks = [pair, turn(pair, sign, 4), turn(pair, -sign, 4), turn(pair, 2, 4)]

    def inner_first(g):
        for p in range(2):
            ref = weights.at[g, p, outer[p], pair, inner[p]]
            send(("i1r", g, p), ref, ref, rights[inner_axis[p]])
            send(("i1l", g, p), ref, ref, lefts[inner_axis[p]])

    def inner_second(g):
        for p in range(2):
            arrived(("i1r", g, p), ("i1l", g, p))
            ref = weights.at[g, p, outer[p], pair]
            low = ref.at[turn(inner[p], -1, 4), pl.ds(0, PAIR_ROWS)]
            high = ref.at[turn(inner[p], 1, 4), pl.ds(PAIR_ROWS, PAIR_ROWS)]
            send(("i2r", g, p), low, low, rights[inner_axis[p]])
            send(("i2l", g, p), high, high, lefts[inner_axis[p]])

    def inner_done(g):
        for p in range(2):
            arrived(("i2r", g, p), ("i2l", g, p))

    def z_step(step, g):
        half = (1 - odd) if step == 3 else odd
        for p in range(2):
            if step >= 2:
                arrived(("z", step - 1, g, p))
            ref = weights.at[g, p, outer[p], blocks[step - 1]]
            if step >= 3:
                ref = ref.at[pl.ds(half * 2, 2)]
            send(("z", step, g, p), ref, ref, inter if step % 2 else intra)

    def z_done(g):
        for p in range(2):
            arrived(("z", 4, g, p))

    def outer_first(block, g):
        for p in range(2):
            ref = weights.at[g, p, outer[p], blocks[block]]
            send(("o1r", block, g, p), ref, ref, rights[outer_axis[p]])
            send(("o1l", block, g, p), ref, ref, lefts[outer_axis[p]])

    def outer_second(block, g):
        for p in range(2):
            arrived(("o1r", block, g, p), ("o1l", block, g, p))
            low = weights.at[g, p, turn(outer[p], -1, 4), blocks[block], pl.ds(0, 2)]
            high = weights.at[g, p, turn(outer[p], 1, 4), blocks[block], pl.ds(2, 2)]
            send(("o2r", block, g, p), low, low, rights[outer_axis[p]])
            send(("o2l", block, g, p), high, high, lefts[outer_axis[p]])

    def outer_done(g):
        for block in range(4):
            for p in range(2):
                arrived(("o2r", block, g, p), ("o2l", block, g, p))

    def project(g):
        acc[...] = jnp.zeros_like(acc)

        @pl.loop(0, 4)
        def _(yy):
            left = acts[:, pl.ds(pl.multiple_of(yy * 1280, 1280), 1280)]
            for p in range(2):
                tiles = []
                for t in range(2):
                    pieces = []
                    for zh in range(2):
                        for xx in range(4):
                            for zl in range(2):
                                place = (yy, xx) if p == 0 else (xx, yy)
                                pieces.append(
                                    weights[
                                        g,
                                        p,
                                        place[0],
                                        zh * 2 + zl,
                                        place[1],
                                        pl.ds(t * PAIR_ROWS, PAIR_ROWS),
                                    ]
                                )
                    tiles.append(jnp.concatenate(pieces, axis=0))
                acc[p] += jnp.dot(
                    left, jnp.concatenate(tiles, axis=1), preferred_element_type=F32
                )

    def store_pages(g, head, fields):
        scales = jnp.zeros((16, LANES), F32)
        line = lax.broadcasted_iota(jnp.int32, (16, LANES), 0)
        for page in range(4):
            largest = jnp.max(jnp.abs(fields[page]), axis=(0, 1), keepdims=True)
            scale = ((largest + 1e-06) / 448.0).astype(BF16).astype(F32)
            stage[g, head, pl.ds(page * PAGE, PAGE)] = (fields[page] / scale).astype(BF16)
            scales = jnp.where(line == page, scale, scales)
        stage[g, head, pl.ds(CHIP_TOKENS, 16)] = scales.astype(BF16)

    def all_to_all(g):
        for d in range(3):
            send(
                ("a2a", g, d), stage.at[g, far_chips[d]], pool_ref.at[1 - g, z_lo], columns[d]
            )
        own = pltpu.make_async_copy(
            stage.at[g, z_lo], pool_ref.at[1 - g, z_lo], local_sem.at[2 + g]
        )
        own.start()
        return own

    def values():
        project(0)
        for head in range(4):
            p, lanes = head // 2, pl.ds(head % 2 * LANES, LANES)
            pages = []
            for page in range(4):
                part = pl.ds(page * PAGE, PAGE)
                pages.append(jnp.where(live_ref[part] > 0.5, acc[p, part, lanes], 0.0))
            store_pages(0, head, pages)
        tail = pl.ds(CHIP_TOKENS, FRESH)
        for head in range(4):
            p, lanes = head // 2, pl.ds(head % 2 * LANES, LANES)

            @pl.when(z_lo == head)
            def _():
                fresh_ref[1] = acc[p, tail, lanes].astype(BF16)

    def keys():
        project(1)
        total = jnp.zeros((ROWS, 1), F32)
        for p in range(2):
            total += jnp.sum(acc[p] * acc[p], axis=1, keepdims=True)
        squares[0] = jnp.broadcast_to(total, (ROWS, LANES))
        send("squares", squares.at[0], squares.at[1], sibling)
        arrived("squares")
        squares[1] = lax.rsqrt((squares[0] + squares[1]) * (1.0 / (HEADS * HEAD)) + 1e-06)

        def turned(head, part):
            p, lanes = head // 2, pl.ds(head % 2 * LANES, LANES)
            gain = gain_ref[pl.ds(head * 2 + core, 1), :]
            row = acc[p, part, lanes] * squares[1, part] * gain
            return row * cos_ref[part] + pltpu.roll(row, 64, 1) * sin_ref[part]

        for head in range(4):
            pages = []
            for page in range(4):
                part = pl.ds(page * PAGE, PAGE)
                pages.append(jnp.where(live_ref[part] > 0.5, turned(head, part), 0.0))
            store_pages(1, head, pages)
        tail = pl.ds(CHIP_TOKENS, FRESH)
        for head in range(4):

            @pl.when(z_lo == head)
            def _():
                fresh_ref[0] = turned(head, tail).astype(BF16)

    V, K = 0, 1
    inner_first(V)
    inner_first(K)
    inner_second(V)
    inner_second(K)
    inner_done(V)
    z_step(1, V)
    outer_first(0, V)
    inner_done(K)
    z_step(1, K)
    outer_first(0, K)
    outer_second(0, V)
    outer_second(0, K)
    z_step(2, V)
    outer_first(1, V)
    z_step(2, K)
    outer_first(1, K)
    outer_second(1, V)
    z_step(3, V)
    outer_first(2, V)
    outer_second(1, K)
    z_step(3, K)
    outer_first(2, K)
    outer_second(2, V)
    z_step(4, V)
    z_done(V)
    outer_first(3, V)
    outer_second(2, K)
    z_step(4, K)
    z_done(K)
    outer_first(3, K)
    outer_second(3, V)
    outer_second(3, K)
    own_acts.wait()
    own_decode.wait()
    arrived("acts")
    outer_done(V)
    values()
    own_values = all_to_all(V)
    outer_done(K)
    keys()
    own_keys = all_to_all(K)
    own_values.wait()
    own_keys.wait()
    for g in range(2):
        for d in range(3):
            arrived(("a2a", g, d))
    for copy in copies.values():
        copy.wait_send()


N_COPIES = 4 + 4 * 24 + 1 + 6


def attend_expand(place_ref, q_ref, near_ref, far_ref, fresh_ref, out_ref, fork_ref, weight):
    factor = 1.0 / math.sqrt(HEAD)
    steps = 3
    rows = GROUP * steps * 8
    lane = lax.broadcasted_iota(jnp.int32, (1, LANES), 1)
    r = lax.broadcasted_iota(jnp.int32, (rows, steps * 8), 0)
    c = lax.broadcasted_iota(jnp.int32, (rows, steps * 8), 1)
    visible = (jnp.bitwise_and(r, 7) == jnp.bitwise_and(c, 7)) & (
        jnp.right_shift(lax.rem(r, steps * 8), 3) >= jnp.right_shift(c, 3)
    )
    results = []
    for side, pool in enumerate((near_ref, far_ref)):
        samples = slice(side * 8, side * 8 + 8)
        query = jnp.concatenate(
            [
                q_ref[:, samples, g * HEAD : (g + 1) * HEAD].astype(F32).reshape(steps * 8, HEAD)
                for g in range(GROUP)
            ],
            axis=0,
        ).astype(BF16)
        new = [
            fresh_ref[kind]
            .astype(F32)
            .reshape(steps, 16, HEAD)[:, samples]
            .reshape(steps * 8, HEAD)
            .astype(BF16)
            for kind in range(2)
        ]
        length = place_ref[side, 16]
        sums = jnp.zeros((rows, LANES), F32)
        for page in range(16):
            chip, part = page // 4, page % 4
            keys = pool[0, chip, part * PAGE : (part + 1) * PAGE]
            scale = pool[0, chip, CHIP_TOKENS : CHIP_TOKENS + 16].astype(F32)[part : part + 1]
            raw = lax.dot_general(
                query, keys, (((1,), (1,)), ((), ())), preferred_element_type=F32
            )
            live = place_ref[side, page] * PAGE + lane < length
            cached = jnp.where(live, jnp.exp(raw * scale * factor), 0.0)
            weight[:, page * PAGE : (page + 1) * PAGE] = cached
            sums += cached
        fresh_raw = lax.dot_general(
            query, new[0], (((1,), (1,)), ((), ())), preferred_element_type=F32
        )
        fresh = jnp.where(visible, jnp.exp(fresh_raw * factor), 0.0)
        total = jnp.sum(sums, axis=1, keepdims=True) + jnp.sum(fresh, axis=1, keepdims=True)
        result = jnp.dot(
            (fresh / total).astype(BF16), new[1], preferred_element_type=F32
        )
        for page in range(16):
            chip, part = page // 4, page % 4
            scale = pool[1, chip, CHIP_TOKENS : CHIP_TOKENS + 16].astype(F32)[part : part + 1]
            portion = weight[:, page * PAGE : (page + 1) * PAGE] / total * scale
            result += jnp.dot(
                portion.astype(BF16),
                pool[1, chip, part * PAGE : (part + 1) * PAGE],
                preferred_element_type=F32,
            )
        results.append(result)
    for g in range(GROUP):
        span = slice(g * steps * 8, (g + 1) * steps * 8)
        both = jnp.concatenate(
            [piece[span].reshape(steps, 8, HEAD) for piece in results], axis=1
        )
        out_ref[:, :, g * HEAD : (g + 1) * HEAD] = both.astype(BF16)
    for kind in range(2):
        for page in range(16):
            chip, part = page // 4, page % 4
            scale = far_ref[kind, chip, CHIP_TOKENS : CHIP_TOKENS + 16].astype(F32)[
                part : part + 1
            ]
            fork_ref[0, kind, page * PAGE : (page + 1) * PAGE] = (
                far_ref[kind, chip, part * PAGE : (part + 1) * PAGE].astype(F32) * scale
            )


def on_device(
    prompt_hidden,
    key_value_weight,
    key_norm_gain,
    page_table,
    lengths,
    source_replica,
    decode_hidden,
    queries,
):
    steps, paired, width = queries.shape
    seq_at = lax.axis_index("seq")
    replica = lax.axis_index("dp")
    replicas = lax.axis_size("dp")
    partner = source_replica[replica]
    own_length = lengths[replica]
    far_length = lengths[partner]

    split = key_value_weight.reshape(SHARD, 2, 4, 2, HEAD)[:, ::-1]
    split = split.transpose(3, 0, 1, 2, 4).reshape(2, SHARD, 8 * HEAD)
    split = jnp.pad(split, ((0, 0), (0, PADDED - SHARD), (0, 0)))

    pages = lax.dynamic_slice(page_table, (replica, seq_at // 2 * 4), (1, 4))[0]
    places = (pages[:, None] * PAGE + jnp.arange(PAGE, dtype=jnp.int32)).reshape(-1)
    starts = jnp.where(jnp.arange(paired) < paired // 2, own_length, far_length)
    new_places = (starts[None, :] + jnp.arange(steps, dtype=jnp.int32)[:, None]).reshape(-1)
    half = HEAD // 2
    freq = 500000.0 ** (-jnp.arange(half, dtype=F32) * 2.0 / HEAD)
    angle = jnp.concatenate([places, new_places]).astype(F32)[:, None] * freq
    cosine, sine = jnp.cos(angle), jnp.sin(angle)
    cosine = jnp.concatenate([cosine, cosine], axis=1)
    sine = jnp.concatenate([-sine, sine], axis=1)
    live = jnp.broadcast_to((places < own_length)[:, None], (CHIP_TOKENS, LANES)).astype(F32)

    vmem = pl.BlockSpec(memory_space=pltpu.VMEM)
    hbm = pl.BlockSpec(memory_space=pl.ANY)
    pool, fresh = pl.pallas_call(
        gather_project,
        out_shape=(
            jax.ShapeDtypeStruct((2, 4, SLAB, LANES), BF16),
            jax.ShapeDtypeStruct((2, FRESH, LANES), BF16),
        ),
        in_specs=[vmem, hbm, hbm, vmem, vmem, vmem, vmem],
        out_specs=(hbm, vmem),
        scratch_shapes=[
            pltpu.VMEM((4, PADDED, 8 * LANES), BF16),
            pltpu.VMEM((ROWS, WIDTH), BF16),
            pltpu.VMEM((2, 2, 4, 4, 4, BLOCK, LANES), BF16),
            pltpu.VMEM((2, ROWS, 2 * LANES), F32),
            pltpu.VMEM((2, 4, SLAB, LANES), BF16),
            pltpu.VMEM((2, ROWS, LANES), F32),
            pltpu.SemaphoreType.DMA((N_COPIES,)),
            pltpu.SemaphoreType.DMA((N_COPIES,)),
            pltpu.SemaphoreType.DMA((4,)),
        ],
        compiler_params=pltpu.CompilerParams(
            collective_id=0, has_side_effects=True, vmem_limit_bytes=44 * 1024 * 1024
        ),
    )(
        split,
        prompt_hidden[0],
        decode_hidden.reshape(steps * paired, WIDTH),
        cosine,
        sine,
        live,
        key_norm_gain.reshape(HEADS, HEAD),
    )

    def swap(mask):
        def branch(array):
            return lax.ppermute(array, "dp", [(i, i ^ mask) for i in range(replicas)])

        return branch

    mask = jnp.bitwise_xor(partner, replica)
    far_pool = lax.switch(mask - 1, [swap(m) for m in range(1, replicas)], pool)

    table = jnp.stack([page_table[replica], page_table[partner]])
    place = jnp.concatenate([table, jnp.stack([own_length, far_length])[:, None]], axis=1)
    smem = pl.BlockSpec(memory_space=pltpu.SMEM)
    attended, forked = pl.pallas_call(
        attend_expand,
        out_shape=(
            jax.ShapeDtypeStruct((steps, paired, width), BF16),
            jax.ShapeDtypeStruct((1, 2, 2048, LANES), F32),
        ),
        in_specs=[smem, vmem, vmem, vmem, vmem],
        out_specs=(vmem, vmem),
        scratch_shapes=[pltpu.VMEM((GROUP * steps * 8, 2048), F32)],
        compiler_params=pltpu.CompilerParams(vmem_limit_bytes=32 * 1024 * 1024),
    )(place, queries, pool, far_pool, fresh)
    return attended, forked


def solution(mesh):
    return jax.shard_map(
        on_device,
        mesh=mesh,
        in_specs=(
            P("dp", "seq", None),
            P(("dp", "seq"), None),
            P(),
            P(),
            P(),
            P(),
            P(None, "dp", None),
            P(None, "dp", "seq"),
        ),
        out_specs=(P(None, "dp", "seq"), P("dp", None, None, "seq")),
        check_vma=False,
    )
```

```python
import functools
import math

import jax
import jax.numpy as jnp
import numpy as np
from jax import lax
from jax.experimental import pallas as pl
from jax.experimental.pallas import tpu as pltpu
from jax.sharding import PartitionSpec as P

HEADS = 8
HEAD = 128
PAGE = 128
GROUP = 5
MESH = pl.DeviceIdType.MESH
F32 = jnp.float32
BF16 = jnp.bfloat16

WIDTH = 5120
SHARD = 20
PADDED = 32
PAIR_ROWS = 80
BLOCK = 160
TOKENS = 256
CHIP_TOKENS = 512
FRESH = 48
ROWS = CHIP_TOKENS + FRESH
SLAB = CHIP_TOKENS + 16
LANES = 128


def trig(angle):
    lane = lax.broadcasted_iota(jnp.int32, angle.shape, 1)
    return jnp.cos(angle), jnp.where(lane < HEAD // 2, -jnp.sin(angle), jnp.sin(angle))


def gather_project(
    w_ref,
    prompt_ref,
    decode_ref,
    table_ref,
    length_ref,
    source_ref,
    freq_ref,
    gain_ref,
    pool_ref,
    stage_ref,
    fresh_ref,
    split,
    raw,
    acts,
    weights,
    acc,
    stage,
    squares,
    turns,
    send_sem,
    recv_sem,
    local_sem,
):
    dp = lax.axis_index("dp")
    seq = lax.axis_index("seq")
    core = lax.rem(seq, 2)
    z_lo = seq // 2
    x = lax.rem(dp, 4)
    z_hi = lax.rem(dp // 4, 2)
    y = dp // 8
    z = z_hi * 4 + z_lo
    pair = z // 2
    odd = lax.rem(z, 2)

    def at(yy, zz, xx, cc):
        return (yy * 8 + (zz // 4) * 4 + xx, lax.rem(zz, 4) * 2 + cc)

    def turn(index, by, size):
        return lax.rem(index + (by + size), size)

    sibling = at(y, z, x, 1 - core)
    inter_z = turn(z, 2 * odd - 1, 8)
    intra_z = z + 1 - 2 * odd
    inter = at(y, inter_z, x, core)
    intra = at(y, intra_z, x, core)
    intra_other = at(y, intra_z, x, 1 - core)
    rights = {"x": at(y, z, turn(x, 1, 4), core), "y": at(turn(y, 1, 4), z, x, core)}
    lefts = {"x": at(y, z, turn(x, -1, 4), core), "y": at(turn(y, -1, 4), z, x, core)}
    far_chips = [jnp.bitwise_xor(z_lo, d) for d in (1, 2, 3)]
    columns = [(dp, chip * 2 + core) for chip in far_chips]

    peers = [
        sibling,
        inter,
        intra,
        intra_other,
        rights["x"],
        lefts["x"],
        rights["y"],
        lefts["y"],
        columns[1],
        columns[2],
    ]
    barrier = pltpu.get_barrier_semaphore()
    for peer in peers:
        pl.semaphore_signal(barrier, inc=1, device_id=peer, device_id_type=MESH)

    own_acts = pltpu.make_async_copy(
        prompt_ref.at[0],
        acts.at[pl.ds(pl.multiple_of(core * TOKENS, TOKENS), TOKENS)],
        local_sem.at[0],
    )
    own_acts.start()
    own_decode = [
        pltpu.make_async_copy(
            decode_ref.at[step], acts.at[pl.ds(CHIP_TOKENS + step * 16, 16)], local_sem.at[1 + step]
        )
        for step in range(3)
    ]
    for copy in own_decode:
        copy.start()

    keep = jnp.where(
        lax.broadcasted_iota(jnp.int32, (PADDED, SHARD), 0)
        == lax.broadcasted_iota(jnp.int32, (PADDED, SHARD), 1),
        1.0,
        0.0,
    ).astype(BF16)
    for c in range(2):
        tiles = [
            w_ref[:, pl.ds((1 - g) * HEADS * HEAD + (2 * i + c) * HEAD, HEAD)]
            for g in range(2)
            for i in range(4)
        ]
        split[c] = jnp.dot(
            keep, jnp.concatenate(tiles, axis=1), preferred_element_type=F32
        ).astype(BF16)
    raw[odd * 2 + core] = split[core]
    pl.semaphore_wait(barrier, len(peers))

    number = [0]
    copies = {}

    def send(key, src, dst, device):
        k = number[0]
        number[0] += 1
        copy = pltpu.make_async_remote_copy(
            src_ref=src,
            dst_ref=dst,
            send_sem=send_sem.at[k],
            recv_sem=recv_sem.at[k],
            device_id=device,
            device_id_type=MESH,
        )
        copy.start()
        copies[key] = copy

    def arrived(*keys):
        for key in keys:
            copies[key].wait_recv()

    slot = odd * 2 + core
    mine = split.at[core]
    other = split.at[1 - core]
    send("w_intra", mine, raw.at[slot], intra)
    send("w_other", other, raw.at[slot], intra_other)
    send("w_sibling", other, raw.at[slot], sibling)

    here = pl.ds(pl.multiple_of(core * TOKENS, TOKENS), TOKENS)
    send("acts", prompt_ref.at[0], acts.at[here], sibling)

    arrived("w_intra", "w_other", "w_sibling")
    row = lax.broadcasted_iota(jnp.int32, (PAIR_ROWS, 4 * PADDED), 0)
    col = lax.broadcasted_iota(jnp.int32, (PAIR_ROWS, 4 * PADDED), 1)
    inside = jnp.bitwise_and(col, PADDED - 1)
    source = jnp.right_shift(col, 5)
    pick = jnp.where((row == source * SHARD + inside) & (inside < SHARD), 1.0, 0.0).astype(BF16)
    rows = jnp.dot(
        pick, raw[...].reshape(4 * PADDED, 8 * LANES), preferred_element_type=F32
    ).astype(BF16)

    outer = (y, x)
    inner = (x, y)
    inner_axis = ("x", "y")
    outer_axis = ("y", "x")
    for g in range(2):
        for p in range(2):
            for t in range(2):
                tile = g * 4 + p * 2 + t
                weights[g, p, outer[p], pair, inner[p], pl.ds(t * PAIR_ROWS, PAIR_ROWS)] = rows[
                    :, tile * LANES : (tile + 1) * LANES
                ]

    sign = 2 * odd - 1
    blocks = [pair, turn(pair, sign, 4), turn(pair, -sign, 4), turn(pair, 2, 4)]

    def inner_first(g):
        for p in range(2):
            ref = weights.at[g, p, outer[p], pair, inner[p]]
            send(("i1r", g, p), ref, ref, rights[inner_axis[p]])
            send(("i1l", g, p), ref, ref, lefts[inner_axis[p]])

    def inner_second(g):
        for p in range(2):
            arrived(("i1r", g, p), ("i1l", g, p))
            ref = weights.at[g, p, outer[p], pair]
            low = ref.at[turn(inner[p], -1, 4), pl.ds(0, PAIR_ROWS)]
            high = ref.at[turn(inner[p], 1, 4), pl.ds(PAIR_ROWS, PAIR_ROWS)]
            send(("i2r", g, p), low, low, rights[inner_axis[p]])
            send(("i2l", g, p), high, high, lefts[inner_axis[p]])

    def inner_done(g):
        for p in range(2):
            arrived(("i2r", g, p), ("i2l", g, p))

    def z_step(step, g):
        half = (1 - odd) if step == 3 else odd
        for p in range(2):
            if step >= 2:
                arrived(("z", step - 1, g, p))
            ref = weights.at[g, p, outer[p], blocks[step - 1]]
            if step >= 3:
                ref = ref.at[pl.ds(half * 2, 2)]
            send(("z", step, g, p), ref, ref, inter if step % 2 else intra)

    def z_done(g):
        for p in range(2):
            arrived(("z", 4, g, p))

    def outer_first(block, g):
        for p in range(2):
            ref = weights.at[g, p, outer[p], blocks[block]]
            send(("o1r", block, g, p), ref, ref, rights[outer_axis[p]])
            send(("o1l", block, g, p), ref, ref, lefts[outer_axis[p]])

    def outer_second(block, g):
        for p in range(2):
            arrived(("o1r", block, g, p), ("o1l", block, g, p))
            low = weights.at[g, p, turn(outer[p], -1, 4), blocks[block], pl.ds(0, 2)]
            high = weights.at[g, p, turn(outer[p], 1, 4), blocks[block], pl.ds(2, 2)]
            send(("o2r", block, g, p), low, low, rights[outer_axis[p]])
            send(("o2l", block, g, p), high, high, lefts[outer_axis[p]])

    offsets = (0, -1, 1, 2)

    def own_first(part, g):
        for p in range(2):
            ref = weights.at[g, p, outer[p], pair, turn(inner[p], offsets[part], 4)]
            send(("q1r", part, g, p), ref, ref, rights[outer_axis[p]])
            send(("q1l", part, g, p), ref, ref, lefts[outer_axis[p]])

    def own_second(part, g):
        for p in range(2):
            arrived(("q1r", part, g, p), ("q1l", part, g, p))
            at_part = turn(inner[p], offsets[part], 4)
            low = weights.at[g, p, turn(outer[p], -1, 4), pair, at_part, pl.ds(0, PAIR_ROWS)]
            high = weights.at[
                g, p, turn(outer[p], 1, 4), pair, at_part, pl.ds(PAIR_ROWS, PAIR_ROWS)
            ]
            send(("q2r", part, g, p), low, low, rights[outer_axis[p]])
            send(("q2l", part, g, p), high, high, lefts[outer_axis[p]])

    def outer_done(g):
        for p in range(2):
            if g == 0:
                for part in range(4):
                    arrived(("q2r", part, g, p), ("q2l", part, g, p))
            for block in range(1 - g, 4):
                arrived(("o2r", block, g, p), ("o2l", block, g, p))

    def project(g):
        acc[...] = jnp.zeros_like(acc)

        @pl.loop(0, 4)
        def _(yy):
            left = acts[:, pl.ds(pl.multiple_of(yy * 1280, 1280), 1280)]
            for p in range(2):
                tiles = []
                for t in range(2):
                    pieces = []
                    for zh in range(2):
                        for xx in range(4):
                            for zl in range(2):
                                place = (yy, xx) if p == 0 else (xx, yy)
                                pieces.append(
                                    weights[
                                        g,
                                        p,
                                        place[0],
                                        zh * 2 + zl,
                                        place[1],
                                        pl.ds(t * PAIR_ROWS, PAIR_ROWS),
                                    ]
                                )
                    tiles.append(jnp.concatenate(pieces, axis=0))
                acc[p] += jnp.dot(
                    left, jnp.concatenate(tiles, axis=1), preferred_element_type=F32
                )

    def store_pages(g, head, fields):
        scales = jnp.zeros((16, LANES), F32)
        line = lax.broadcasted_iota(jnp.int32, (16, LANES), 0)
        for page in range(4):
            largest = jnp.max(jnp.abs(fields[page]), axis=(0, 1), keepdims=True)
            scale = ((largest + 1e-06) / 448.0).astype(BF16).astype(F32)
            stage[g, head, pl.ds(page * PAGE, PAGE)] = (fields[page] / scale).astype(BF16)
            scales = jnp.where(line == page, scale, scales)
        stage[g, head, pl.ds(CHIP_TOKENS, 16)] = scales.astype(BF16)

    def all_to_all(g):
        for d in range(3):
            send(
                ("a2a", g, d), stage.at[g, far_chips[d]], pool_ref.at[z_lo], columns[d]
            )
        own = pltpu.make_async_copy(stage.at[g, z_lo], pool_ref.at[z_lo], local_sem.at[4])
        own.start()
        return own

    line = lax.broadcasted_iota(jnp.int32, (PAGE, LANES), 0)
    first = [table_ref[z_lo * 4 + page, dp] * PAGE for page in range(4)]
    own_length = length_ref[dp]

    def live(page):
        return first[page] + line < own_length

    def angles():
        for page in range(4):
            angle = (first[page] + line).astype(F32) * freq_ref[...]
            part = pl.ds(page * PAGE, PAGE)
            turns[0, part], turns[1, part] = trig(angle)
        row = lax.broadcasted_iota(jnp.int32, (FRESH, LANES), 0)
        far_length = length_ref[source_ref[dp]]
        start = jnp.where(jnp.bitwise_and(row, 15) < 8, own_length, far_length)
        angle = (start + jnp.right_shift(row, 4)).astype(F32) * freq_ref[...]
        part = pl.ds(CHIP_TOKENS, FRESH)
        turns[0, part], turns[1, part] = trig(angle)

    def values():
        project(0)
        for head in range(4):
            p, lanes = head // 2, pl.ds(head % 2 * LANES, LANES)
            pages = []
            for page in range(4):
                part = pl.ds(page * PAGE, PAGE)
                pages.append(jnp.where(live(page), acc[p, part, lanes], 0.0))
            store_pages(0, head, pages)
        tail = pl.ds(CHIP_TOKENS, FRESH)
        for head in range(4):
            p, lanes = head // 2, pl.ds(head % 2 * LANES, LANES)

            @pl.when(z_lo == head)
            def _():
                fresh_ref[1] = acc[p, tail, lanes].astype(BF16)

    def keys():
        project(1)
        total = jnp.zeros((ROWS, 1), F32)
        for p in range(2):
            total += jnp.sum(acc[p] * acc[p], axis=1, keepdims=True)
        squares[0] = jnp.broadcast_to(total, (ROWS, LANES))
        send("squares", squares.at[0], squares.at[1], sibling)
        arrived("squares")
        squares[1] = lax.rsqrt((squares[0] + squares[1]) * (1.0 / (HEADS * HEAD)) + 1e-06)

        def turned(head, part):
            p, lanes = head // 2, pl.ds(head % 2 * LANES, LANES)
            gain = gain_ref[pl.ds(head * 2 + core, 1), :]
            row = acc[p, part, lanes] * squares[1, part] * gain
            return row * turns[0, part] + pltpu.roll(row, 64, 1) * turns[1, part]

        for head in range(4):
            pages = []
            for page in range(4):
                part = pl.ds(page * PAGE, PAGE)
                pages.append(jnp.where(live(page), turned(head, part), 0.0))
            store_pages(1, head, pages)
        tail = pl.ds(CHIP_TOKENS, FRESH)
        for head in range(4):

            @pl.when(z_lo == head)
            def _():
                fresh_ref[0] = turned(head, tail).astype(BF16)

    V, K = 0, 1
    inner_first(V)
    own_first(0, V)
    inner_first(K)
    inner_second(V)
    own_first(1, V)
    own_first(2, V)
    inner_second(K)
    inner_done(V)
    z_step(1, V)
    own_first(3, V)
    inner_done(K)
    z_step(1, K)
    outer_first(0, K)
    for part in range(4):
        own_second(part, V)
    angles()
    outer_second(0, K)
    z_step(2, V)
    outer_first(1, V)
    outer_second(1, V)
    z_step(3, V)
    outer_first(2, V)
    z_step(2, K)
    outer_first(1, K)
    outer_second(2, V)
    z_step(4, V)
    z_done(V)
    outer_first(3, V)
    outer_second(1, K)
    z_step(3, K)
    outer_first(2, K)
    outer_second(3, V)
    z_step(4, K)
    z_done(K)
    outer_first(3, K)
    outer_second(2, K)
    own_acts.wait()
    for copy in own_decode:
        copy.wait()
    arrived("acts")
    outer_done(V)
    values()
    own_values = all_to_all(V)
    outer_second(3, K)
    stage_values = pltpu.make_async_copy(stage.at[0], stage_ref.at[0], local_sem.at[5])
    stage_values.start()
    outer_done(K)
    keys()
    stage_keys = pltpu.make_async_copy(stage.at[1], stage_ref.at[1], local_sem.at[6])
    stage_keys.start()
    own_values.wait()
    stage_values.wait()
    stage_keys.wait()
    for d in range(3):
        arrived(("a2a", V, d))
    for copy in copies.values():
        copy.wait_send()


N_COPIES = 4 + 4 * 24 + 2 * 12 + 1 + 3


ATTEND_ROWS = GROUP * 3 * 8


def attend(side, q_ref, keys_ref, values_ref, fresh_ref, page_at, length, weight):
    factor = 1.0 / math.sqrt(HEAD)
    steps = 3
    lane = lax.broadcasted_iota(jnp.int32, (1, LANES), 1)
    r = lax.broadcasted_iota(jnp.int32, (ATTEND_ROWS, steps * 8), 0)
    c = lax.broadcasted_iota(jnp.int32, (ATTEND_ROWS, steps * 8), 1)
    visible = (jnp.bitwise_and(r, 7) == jnp.bitwise_and(c, 7)) & (
        jnp.right_shift(lax.rem(r, steps * 8), 3) >= jnp.right_shift(c, 3)
    )
    samples = slice(side * 8, side * 8 + 8)
    query = jnp.concatenate(
        [
            q_ref[:, samples, g * HEAD : (g + 1) * HEAD].astype(F32).reshape(steps * 8, HEAD)
            for g in range(GROUP)
        ],
        axis=0,
    ).astype(BF16)
    new = [
        fresh_ref[kind]
        .astype(F32)
        .reshape(steps, 16, HEAD)[:, samples]
        .reshape(steps * 8, HEAD)
        .astype(BF16)
        for kind in range(2)
    ]
    sums = jnp.zeros((ATTEND_ROWS, LANES), F32)
    for page in range(16):
        chip, part = page // 4, page % 4
        keys = keys_ref[chip, part * PAGE : (part + 1) * PAGE]
        scale = keys_ref[chip, CHIP_TOKENS : CHIP_TOKENS + 16].astype(F32)[part : part + 1]
        raw = lax.dot_general(query, keys, (((1,), (1,)), ((), ())), preferred_element_type=F32)
        live = page_at(page) * PAGE + lane < length
        cached = jnp.where(live, jnp.exp(raw * scale * factor), 0.0)
        weight[:, page * PAGE : (page + 1) * PAGE] = cached
        sums += cached
    fresh_raw = lax.dot_general(
        query, new[0], (((1,), (1,)), ((), ())), preferred_element_type=F32
    )
    fresh = jnp.where(visible, jnp.exp(fresh_raw * factor), 0.0)
    total = jnp.sum(sums, axis=1, keepdims=True) + jnp.sum(fresh, axis=1, keepdims=True)
    result = jnp.dot((fresh / total).astype(BF16), new[1], preferred_element_type=F32)
    for page in range(16):
        chip, part = page // 4, page % 4
        scale = values_ref[chip, CHIP_TOKENS : CHIP_TOKENS + 16].astype(F32)[part : part + 1]
        portion = weight[:, page * PAGE : (page + 1) * PAGE] / total * scale
        result += jnp.dot(
            portion.astype(BF16),
            values_ref[chip, part * PAGE : (part + 1) * PAGE],
            preferred_element_type=F32,
        )
    return [
        result[g * steps * 8 : (g + 1) * steps * 8].reshape(steps, 8, HEAD) for g in range(GROUP)
    ]


def exchange(
    mask,
    q_ref,
    table_ref,
    length_ref,
    pool_ref,
    stage_ref,
    fresh_ref,
    far_ref,
    near_ref,
    keys,
    weight,
    send_sem,
    recv_sem,
    local_sem,
):
    dp = lax.axis_index("dp")
    seq = lax.axis_index("seq")
    core = lax.rem(seq, 2)
    z_lo = seq // 2
    partner = jnp.bitwise_xor(dp, mask)
    far_chips = [jnp.bitwise_xor(z_lo, d) for d in (1, 2, 3)]
    columns = [(dp, chip * 2 + core) for chip in far_chips]
    partners = [(partner, jnp.bitwise_xor(z_lo, d) * 2 + core) for d in range(4)]
    crosses_z = mask & 4 != 0

    barrier = pltpu.get_barrier_semaphore()
    for peer in columns + partners:
        pl.semaphore_signal(barrier, inc=1, device_id=peer, device_id_type=MESH)
    pl.semaphore_wait(barrier, 7)

    copies = []

    def send(src, dst, device):
        k = len(copies)
        copy = pltpu.make_async_remote_copy(
            src_ref=src,
            dst_ref=dst,
            send_sem=send_sem.at[k],
            recv_sem=recv_sem.at[k],
            device_id=device,
            device_id_type=MESH,
        )
        copy.start()
        copies.append(copy)

    for d in (1, 2, 3):
        send(stage_ref.at[1, far_chips[d - 1]], keys.at[z_lo], columns[d - 1])
    own = pltpu.make_async_copy(stage_ref.at[1, z_lo], keys.at[z_lo], local_sem.at[0])
    own.start()
    if not crosses_z:
        send(pool_ref, far_ref.at[1], partners[0])
    for d in range(4):
        send(stage_ref.at[1, jnp.bitwise_xor(z_lo, d)], far_ref.at[0, z_lo], partners[d])
        if crosses_z:
            send(stage_ref.at[0, jnp.bitwise_xor(z_lo, d)], far_ref.at[1, z_lo], partners[d])
    own.wait()
    for d in range(3):
        copies[d].wait_recv()
    near = attend(
        0,
        q_ref,
        keys,
        pool_ref,
        fresh_ref,
        lambda page: table_ref[page, dp],
        length_ref[dp],
        weight,
    )
    for g in range(GROUP):
        near_ref[:, :, g * HEAD : (g + 1) * HEAD] = near[g]
    for copy in copies[3:]:
        copy.wait_recv()
    for copy in copies:
        copy.wait_send()


def finish(
    q_ref, table_ref, length_ref, source_ref, far_ref, near_ref, fresh_ref, out_ref, fork_ref, weight
):
    partner = source_ref[lax.axis_index("dp")]
    far = attend(
        1,
        q_ref,
        far_ref.at[0],
        far_ref.at[1],
        fresh_ref,
        lambda page: table_ref[page, partner],
        length_ref[partner],
        weight,
    )
    for g in range(GROUP):
        span = slice(g * HEAD, (g + 1) * HEAD)
        out_ref[:, :, span] = jnp.concatenate([near_ref[:, :, span], far[g]], axis=1).astype(BF16)
    for kind in range(2):
        for page in range(16):
            chip, part = page // 4, page % 4
            scale = far_ref[kind, chip, CHIP_TOKENS : CHIP_TOKENS + 16].astype(F32)[
                part : part + 1
            ]
            fork_ref[0, kind, page * PAGE : (page + 1) * PAGE] = (
                far_ref[kind, chip, part * PAGE : (part + 1) * PAGE].astype(F32) * scale
            )


def on_device(
    prompt_hidden,
    key_value_weight,
    key_norm_gain,
    page_table,
    lengths,
    source_replica,
    decode_hidden,
    queries,
):
    steps, paired, width = queries.shape
    replicas = lax.axis_size("dp")
    table = page_table.T
    freq = 500000.0 ** (-np.arange(HEAD // 2) * 2.0 / HEAD)
    freq = jnp.asarray(np.concatenate([freq, freq])[None].astype(np.float32))

    vmem = pl.BlockSpec(memory_space=pltpu.VMEM)
    smem = pl.BlockSpec(memory_space=pltpu.SMEM)
    hbm = pl.BlockSpec(memory_space=pl.ANY)
    pool, stage, fresh = pl.pallas_call(
        gather_project,
        out_shape=(
            jax.ShapeDtypeStruct((4, SLAB, LANES), BF16),
            jax.ShapeDtypeStruct((2, 4, SLAB, LANES), BF16),
            jax.ShapeDtypeStruct((2, FRESH, LANES), BF16),
        ),
        in_specs=[vmem, hbm, hbm, smem, smem, smem, vmem, vmem],
        out_specs=(hbm, hbm, vmem),
        scratch_shapes=[
            pltpu.VMEM((2, PADDED, 8 * LANES), BF16),
            pltpu.VMEM((4, PADDED, 8 * LANES), BF16),
            pltpu.VMEM((ROWS, WIDTH), BF16),
            pltpu.VMEM((2, 2, 4, 4, 4, BLOCK, LANES), BF16),
            pltpu.VMEM((2, ROWS, 2 * LANES), F32),
            pltpu.VMEM((2, 4, SLAB, LANES), BF16),
            pltpu.VMEM((2, ROWS, LANES), F32),
            pltpu.VMEM((2, ROWS, LANES), F32),
            pltpu.SemaphoreType.DMA((N_COPIES,)),
            pltpu.SemaphoreType.DMA((N_COPIES,)),
            pltpu.SemaphoreType.DMA((8,)),
        ],
        compiler_params=pltpu.CompilerParams(
            collective_id=0, has_side_effects=True, vmem_limit_bytes=44 * 1024 * 1024
        ),
    )(
        key_value_weight,
        prompt_hidden,
        decode_hidden,
        table,
        lengths,
        source_replica,
        freq,
        key_norm_gain.reshape(HEADS, HEAD),
    )

    def exchange_by(mask):
        return pl.pallas_call(
            functools.partial(exchange, mask),
            out_shape=(
                jax.ShapeDtypeStruct((2, 4, SLAB, LANES), BF16),
                jax.ShapeDtypeStruct((steps, paired // 2, width), F32),
            ),
            in_specs=[vmem, smem, smem, vmem, hbm, vmem],
            out_specs=(hbm, vmem),
            scratch_shapes=[
                pltpu.VMEM((4, SLAB, LANES), BF16),
                pltpu.VMEM((ATTEND_ROWS, 2048), F32),
                pltpu.SemaphoreType.DMA((11,)),
                pltpu.SemaphoreType.DMA((11,)),
                pltpu.SemaphoreType.DMA((1,)),
            ],
            compiler_params=pltpu.CompilerParams(
                collective_id=mask, has_side_effects=True, vmem_limit_bytes=32 * 1024 * 1024
            ),
        )

    far_pool, near = lax.switch(
        source_replica[0] - 1,
        [exchange_by(mask) for mask in range(1, replicas)],
        queries,
        table,
        lengths,
        pool,
        stage,
        fresh,
    )

    attended, forked = pl.pallas_call(
        finish,
        out_shape=(
            jax.ShapeDtypeStruct((steps, paired, width), BF16),
            jax.ShapeDtypeStruct((1, 2, 2048, LANES), F32),
        ),
        in_specs=[vmem, smem, smem, smem, vmem, vmem, vmem],
        out_specs=(vmem, vmem),
        scratch_shapes=[pltpu.VMEM((ATTEND_ROWS, 2048), F32)],
        compiler_params=pltpu.CompilerParams(vmem_limit_bytes=32 * 1024 * 1024),
    )(queries, table, lengths, source_replica, far_pool, near, fresh)
    return attended, forked


def solution(mesh):
    return jax.shard_map(
        on_device,
        mesh=mesh,
        in_specs=(
            P("dp", "seq", None),
            P(("dp", "seq"), None),
            P(),
            P(),
            P(),
            P(),
            P(None, "dp", None),
            P(None, "dp", "seq"),
        ),
        out_specs=(P(None, "dp", "seq"), P("dp", None, None, "seq")),
        check_vma=False,
    )
```

```python
import functools
import math

import jax
import jax.numpy as jnp
import numpy as np
from jax import lax
from jax.experimental import pallas as pl
from jax.experimental.pallas import tpu as pltpu
from jax.sharding import PartitionSpec as P

HEADS = 8
HEAD = 128
PAGE = 128
GROUP = 5
MESH = pl.DeviceIdType.MESH
F32 = jnp.float32
BF16 = jnp.bfloat16

WIDTH = 5120
SHARD = 20
PADDED = 32
PAIR_ROWS = 80
BLOCK = 160
TOKENS = 256
CHIP_TOKENS = 512
FRESH = 48
ROWS = CHIP_TOKENS + FRESH
SLAB = CHIP_TOKENS + 16
LANES = 128
UPPER = pl.ds(0, 272)
LOWER = pl.ds(272, 256)


def trig(angle):
    lane = lax.broadcasted_iota(jnp.int32, angle.shape, 1)
    return jnp.cos(angle), jnp.where(lane < HEAD // 2, -jnp.sin(angle), jnp.sin(angle))


def gather_project(
    w_hbm,
    prompt_ref,
    decode_ref,
    table_hbm,
    length_hbm,
    source_hbm,
    freq_hbm,
    gain_hbm,
    pool_ref,
    across_ref,
    stage_ref,
    fresh_ref,
    w_ref,
    table_ref,
    length_ref,
    source_ref,
    freq_ref,
    gain_ref,
    split,
    raw,
    acts,
    weights,
    acc,
    stage,
    squares,
    turns,
    relay,
    send_sem,
    recv_sem,
    local_sem,
):
    dp = lax.axis_index("dp")
    seq = lax.axis_index("seq")
    core = lax.rem(seq, 2)
    z_lo = seq // 2
    x = lax.rem(dp, 4)
    z_hi = lax.rem(dp // 4, 2)
    y = dp // 8
    z = z_hi * 4 + z_lo
    pair = z // 2
    odd = lax.rem(z, 2)

    def at(yy, zz, xx, cc):
        return (yy * 8 + (zz // 4) * 4 + xx, lax.rem(zz, 4) * 2 + cc)

    def turn(index, by, size):
        return lax.rem(index + (by + size), size)

    sibling = at(y, z, x, 1 - core)
    inter_z = turn(z, 2 * odd - 1, 8)
    intra_z = z + 1 - 2 * odd
    inter = at(y, inter_z, x, core)
    intra = at(y, intra_z, x, core)
    intra_other = at(y, intra_z, x, 1 - core)
    rights = {"x": at(y, z, turn(x, 1, 4), core), "y": at(turn(y, 1, 4), z, x, core)}
    lefts = {"x": at(y, z, turn(x, -1, 4), core), "y": at(turn(y, -1, 4), z, x, core)}
    far_chips = [jnp.bitwise_xor(z_lo, d) for d in (1, 2, 3)]
    columns = [(dp, chip * 2 + core) for chip in far_chips]
    opposite = [
        (jnp.bitwise_xor(dp, 4), jnp.bitwise_xor(z_lo, d) * 2 + core) for d in range(4)
    ]

    ahead = at(y, turn(z, 2, 8), x, core)
    behind = at(y, turn(z, -2, 8), x, core)

    peers = opposite[1:] + [
        ahead,
        behind,
        sibling,
        inter,
        intra,
        intra_other,
        rights["x"],
        lefts["x"],
        rights["y"],
        lefts["y"],
        columns[1],
        columns[2],
    ]
    barrier = pltpu.get_barrier_semaphore()
    for peer in peers:
        pl.semaphore_signal(barrier, inc=1, device_id=peer, device_id_type=MESH)

    small = [
        pltpu.make_async_copy(src, dst, local_sem.at[8 + k])
        for k, (src, dst) in enumerate(
            [
                (w_hbm, w_ref),
                (table_hbm, table_ref),
                (length_hbm, length_ref),
                (source_hbm, source_ref),
                (freq_hbm, freq_ref),
                (gain_hbm, gain_ref),
            ]
        )
    ]
    for copy in small:
        copy.start()
    own_acts = pltpu.make_async_copy(
        prompt_ref.at[0],
        acts.at[pl.ds(pl.multiple_of(core * TOKENS, TOKENS), TOKENS)],
        local_sem.at[0],
    )
    own_acts.start()
    own_decode = [
        pltpu.make_async_copy(
            decode_ref.at[step], acts.at[pl.ds(CHIP_TOKENS + step * 16, 16)], local_sem.at[1 + step]
        )
        for step in range(3)
    ]
    for copy in own_decode:
        copy.start()

    for copy in small:
        copy.wait()
    keep = jnp.where(
        lax.broadcasted_iota(jnp.int32, (PADDED, SHARD), 0)
        == lax.broadcasted_iota(jnp.int32, (PADDED, SHARD), 1),
        1.0,
        0.0,
    ).astype(BF16)
    for c in range(2):
        tiles = [
            w_ref[:, pl.ds((1 - g) * HEADS * HEAD + (2 * i + c) * HEAD, HEAD)]
            for g in range(2)
            for i in range(4)
        ]
        split[c] = jnp.dot(
            keep, jnp.concatenate(tiles, axis=1), preferred_element_type=F32
        ).astype(BF16)
    raw[odd * 2 + core] = split[core]
    pl.semaphore_wait(barrier, len(peers))

    number = [0]
    copies = {}

    def send(key, src, dst, device):
        k = number[0]
        number[0] += 1
        copy = pltpu.make_async_remote_copy(
            src_ref=src,
            dst_ref=dst,
            send_sem=send_sem.at[k],
            recv_sem=recv_sem.at[k],
            device_id=device,
            device_id_type=MESH,
        )
        copy.start()
        copies[key] = copy

    def arrived(*keys):
        for key in keys:
            copies[key].wait_recv()

    slot = odd * 2 + core
    mine = split.at[core]
    other = split.at[1 - core]
    send("w_intra", mine, raw.at[slot], intra)
    send("w_other", other, raw.at[slot], intra_other)
    send("w_sibling", other, raw.at[slot], sibling)

    here = pl.ds(pl.multiple_of(core * TOKENS, TOKENS), TOKENS)
    send("acts", prompt_ref.at[0], acts.at[here], sibling)

    arrived("w_intra", "w_other", "w_sibling")
    row = lax.broadcasted_iota(jnp.int32, (PAIR_ROWS, 4 * PADDED), 0)
    col = lax.broadcasted_iota(jnp.int32, (PAIR_ROWS, 4 * PADDED), 1)
    inside = jnp.bitwise_and(col, PADDED - 1)
    source = jnp.right_shift(col, 5)
    pick = jnp.where((row == source * SHARD + inside) & (inside < SHARD), 1.0, 0.0).astype(BF16)
    rows = jnp.dot(
        pick, raw[...].reshape(4 * PADDED, 8 * LANES), preferred_element_type=F32
    ).astype(BF16)

    outer = (y, x)
    inner = (x, y)
    inner_axis = ("x", "y")
    outer_axis = ("y", "x")
    for g in range(2):
        for p in range(2):
            for t in range(2):
                tile = g * 4 + p * 2 + t
                weights[g, p, outer[p], pair, inner[p], pl.ds(t * PAIR_ROWS, PAIR_ROWS)] = rows[
                    :, tile * LANES : (tile + 1) * LANES
                ]

    offsets = (0, -1, 1, 2)
    sign = 2 * odd - 1
    blocks = [pair, turn(pair, sign, 4), turn(pair, -sign, 4), turn(pair, 2, 4)]

    def inner_first(g):
        for p in range(2):
            ref = weights.at[g, p, outer[p], pair, inner[p]]
            send(("i1r", g, p), ref, ref, rights[inner_axis[p]])
            send(("i1l", g, p), ref, ref, lefts[inner_axis[p]])

    def inner_second(g):
        for p in range(2):
            arrived(("i1r", g, p), ("i1l", g, p))
            ref = weights.at[g, p, outer[p], pair]
            low = ref.at[turn(inner[p], -1, 4), pl.ds(0, PAIR_ROWS)]
            high = ref.at[turn(inner[p], 1, 4), pl.ds(PAIR_ROWS, PAIR_ROWS)]
            send(("i2r", g, p), low, low, rights[inner_axis[p]])
            send(("i2l", g, p), high, high, lefts[inner_axis[p]])

    def inner_done(g):
        for p in range(2):
            arrived(("i2r", g, p), ("i2l", g, p))

    def z_step(step, g):
        half = (1 - odd) if step == 3 else odd
        for p in range(2):
            if step >= 2:
                arrived(("z", step - 1, g, p))
            ref = weights.at[g, p, outer[p], blocks[step - 1]]
            if step >= 3:
                ref = ref.at[pl.ds(half * 2, 2)]
            send(("z", step, g, p), ref, ref, inter if step % 2 else intra)

    def z_part(step, part, g):
        half = (1 - odd) if step == 3 else odd
        for p in range(2):
            at_part = turn(inner[p], offsets[part], 4)
            if step >= 2:
                arrived(("zp", step - 1, part, g, p))
            ref = weights.at[g, p, outer[p], blocks[step - 1], at_part]
            if step >= 3:
                ref = ref.at[pl.ds(pl.multiple_of(half * PAIR_ROWS, 16), PAIR_ROWS)]
            send(("zp", step, part, g, p), ref, ref, inter if step % 2 else intra)

    def z_parts_done(g):
        for part in range(4):
            for p in range(2):
                arrived(("zp", 4, part, g, p))

    def z_done(g):
        for p in range(2):
            arrived(("z", 4, g, p))

    def outer_first(block, g):
        for p in range(2):
            ref = weights.at[g, p, outer[p], blocks[block]]
            send(("o1r", block, g, p), ref, ref, rights[outer_axis[p]])
            send(("o1l", block, g, p), ref, ref, lefts[outer_axis[p]])

    def outer_second(block, g):
        for p in range(2):
            arrived(("o1r", block, g, p), ("o1l", block, g, p))
            low = weights.at[g, p, turn(outer[p], -1, 4), blocks[block], pl.ds(0, 2)]
            high = weights.at[g, p, turn(outer[p], 1, 4), blocks[block], pl.ds(2, 2)]
            send(("o2r", block, g, p), low, low, rights[outer_axis[p]])
            send(("o2l", block, g, p), high, high, lefts[outer_axis[p]])

    def own_first(part, g):
        for p in range(2):
            ref = weights.at[g, p, outer[p], pair, turn(inner[p], offsets[part], 4)]
            send(("q1r", part, g, p), ref, ref, rights[outer_axis[p]])
            send(("q1l", part, g, p), ref, ref, lefts[outer_axis[p]])

    def own_second(part, g):
        for p in range(2):
            arrived(("q1r", part, g, p), ("q1l", part, g, p))
            at_part = turn(inner[p], offsets[part], 4)
            low = weights.at[g, p, turn(outer[p], -1, 4), pair, at_part, pl.ds(0, PAIR_ROWS)]
            high = weights.at[
                g, p, turn(outer[p], 1, 4), pair, at_part, pl.ds(PAIR_ROWS, PAIR_ROWS)
            ]
            send(("q2r", part, g, p), low, low, rights[outer_axis[p]])
            send(("q2l", part, g, p), high, high, lefts[outer_axis[p]])

    def outer_done(g):
        for p in range(2):
            if g == 0:
                for part in range(4):
                    arrived(("q2r", part, g, p), ("q2l", part, g, p))
            for block in range(1 - g, 4):
                arrived(("o2r", block, g, p), ("o2l", block, g, p))

    def project(g):
        acc[...] = jnp.zeros_like(acc)

        @pl.loop(0, 4)
        def _(yy):
            left = acts[:, pl.ds(pl.multiple_of(yy * 1280, 1280), 1280)]
            for p in range(2):
                tiles = []
                for t in range(2):
                    pieces = []
                    for zh in range(2):
                        for xx in range(4):
                            for zl in range(2):
                                place = (yy, xx) if p == 0 else (xx, yy)
                                pieces.append(
                                    weights[
                                        g,
                                        p,
                                        place[0],
                                        zh * 2 + zl,
                                        place[1],
                                        pl.ds(t * PAIR_ROWS, PAIR_ROWS),
                                    ]
                                )
                    tiles.append(jnp.concatenate(pieces, axis=0))
                acc[p] += jnp.dot(
                    left, jnp.concatenate(tiles, axis=1), preferred_element_type=F32
                )

    def pack(g):
        peaks = []
        for head in range(4):
            p, lanes = head // 2, pl.ds(head % 2 * LANES, LANES)
            for page in range(4):
                part = pl.ds(page * PAGE, PAGE)
                peaks.append(jnp.max(jnp.abs(acc[p, part, lanes]), axis=0, keepdims=True))
        largest = jnp.max(jnp.concatenate(peaks, axis=0), axis=1, keepdims=True)
        scale = ((largest + 1e-06) / 448.0).astype(BF16).astype(F32)
        inverse = 1.0 / scale
        row = lax.broadcasted_iota(jnp.int32, (16, LANES), 0)
        for head in range(4):
            p, lanes = head // 2, pl.ds(head % 2 * LANES, LANES)
            rows = jnp.zeros((16, LANES), F32)
            for page in range(4):
                part = pl.ds(page * PAGE, PAGE)
                k = head * 4 + page
                stage[g, head, part] = (acc[p, part, lanes] * inverse[k : k + 1]).astype(BF16)
                rows = jnp.where(row == page, scale[k : k + 1], rows)
            stage[g, head, pl.ds(CHIP_TOKENS, 16)] = rows.astype(BF16)

    def all_to_all(g):
        for d in range(3):
            send(
                ("a2a", g, d), stage.at[g, far_chips[d]], pool_ref.at[z_lo], columns[d]
            )
        send(("ahead", 1), stage.at[g, z_lo, UPPER], relay.at[0, UPPER], ahead)
        send(("behind", 1), stage.at[g, z_lo, LOWER], relay.at[1, pl.ds(0, 256)], behind)
        for d in (1, 2, 3):
            send(
                ("across", d),
                stage.at[g, jnp.bitwise_xor(z_lo, d)],
                across_ref.at[z_lo],
                opposite[d],
            )
        own = pltpu.make_async_copy(stage.at[g, z_lo], pool_ref.at[z_lo], local_sem.at[4])
        own.start()
        return own

    def pass_on():
        arrived(("ahead", 1), ("behind", 1))
        place = jnp.bitwise_xor(z_lo, 2)
        send(("ahead", 2), relay.at[0, UPPER], across_ref.at[place, UPPER], ahead)
        send(("behind", 2), relay.at[1, pl.ds(0, 256)], across_ref.at[place, LOWER], behind)

    line = lax.broadcasted_iota(jnp.int32, (PAGE, LANES), 0)
    first = [table_ref[z_lo * 4 + page, dp] * PAGE for page in range(4)]
    own_length = length_ref[dp]

    def live(page):
        return first[page] + line < own_length

    def angles():
        for page in range(4):
            angle = (first[page] + line).astype(F32) * freq_ref[...]
            part = pl.ds(page * PAGE, PAGE)
            turns[0, part], turns[1, part] = trig(angle)
        row = lax.broadcasted_iota(jnp.int32, (FRESH, LANES), 0)
        far_length = length_ref[source_ref[dp]]
        start = jnp.where(jnp.bitwise_and(row, 15) < 8, own_length, far_length)
        angle = (start + jnp.right_shift(row, 4)).astype(F32) * freq_ref[...]
        part = pl.ds(CHIP_TOKENS, FRESH)
        turns[0, part], turns[1, part] = trig(angle)

    tail = pl.ds(CHIP_TOKENS, FRESH)

    def keep_fresh(kind):
        for head in range(4):
            p, lanes = head // 2, pl.ds(head % 2 * LANES, LANES)

            @pl.when(z_lo == head)
            def _():
                fresh_ref[kind] = acc[p, tail, lanes].astype(BF16)

    def values():
        project(0)
        keep_fresh(1)
        for page in range(4):
            part = pl.ds(page * PAGE, PAGE)
            for head in range(4):
                p, lanes = head // 2, pl.ds(head % 2 * LANES, LANES)
                acc[p, part, lanes] = jnp.where(live(page), acc[p, part, lanes], 0.0)
        pack(0)

    def keys():
        project(1)
        total = jnp.zeros((ROWS, 1), F32)
        for p in range(2):
            total += jnp.sum(acc[p] * acc[p], axis=1, keepdims=True)
        squares[0] = jnp.broadcast_to(total, (ROWS, LANES))
        send("squares", squares.at[0], squares.at[1], sibling)
        pass_on()
        parts = [pl.ds(page * PAGE, PAGE) for page in range(4)] + [tail]
        for head in range(4):
            p, lanes = head // 2, pl.ds(head % 2 * LANES, LANES)
            gain = gain_ref[pl.ds(head * 2 + core, 1), :]
            for part in parts:
                row = acc[p, part, lanes] * gain
                acc[p, part, lanes] = row * turns[0, part] + pltpu.roll(row, 64, 1) * turns[1, part]
        arrived("squares")
        for page, part in enumerate(parts):
            norm = lax.rsqrt((squares[0, part] + squares[1, part]) * (1.0 / (HEADS * HEAD)) + 1e-06)
            if page < 4:
                norm = jnp.where(live(page), norm, 0.0)
            for head in range(4):
                p, lanes = head // 2, pl.ds(head % 2 * LANES, LANES)
                acc[p, part, lanes] = acc[p, part, lanes] * norm
        keep_fresh(0)
        pack(1)

    V, K = 0, 1
    inner_first(V)
    z_part(1, 0, V)
    own_first(0, V)
    z_part(1, 0, K)
    inner_first(K)
    inner_second(V)
    z_part(1, 1, V)
    z_part(1, 2, V)
    own_first(1, V)
    own_first(2, V)
    z_part(2, 0, V)
    own_second(0, V)
    inner_done(V)
    z_part(1, 3, V)
    own_first(3, V)
    z_part(2, 0, K)
    own_second(1, V)
    own_second(2, V)
    z_part(3, 0, V)
    z_part(2, 1, V)
    inner_second(K)
    own_second(3, V)
    z_part(2, 2, V)
    z_part(3, 0, K)
    inner_done(K)
    outer_first(0, K)
    z_part(1, 1, K)
    z_part(3, 1, V)
    z_part(2, 3, V)
    outer_first(1, V)
    angles()
    z_part(4, 0, V)
    z_part(3, 2, V)
    z_part(4, 0, K)
    z_part(1, 2, K)
    z_part(3, 3, V)
    outer_first(2, V)
    z_part(2, 1, K)
    z_part(4, 1, V)
    z_part(4, 2, V)
    z_part(1, 3, K)
    z_part(2, 2, K)
    z_part(3, 1, K)
    outer_second(1, V)
    z_part(4, 3, V)
    z_part(2, 3, K)
    z_part(3, 2, K)
    z_part(4, 1, K)
    outer_second(2, V)
    z_parts_done(V)
    outer_first(3, V)
    z_part(4, 2, K)
    z_part(3, 3, K)
    z_part(4, 3, K)
    outer_second(0, K)
    outer_second(3, V)
    outer_first(1, K)
    own_acts.wait()
    for copy in own_decode:
        copy.wait()
    arrived("acts")
    outer_done(V)
    values()
    outer_second(1, K)
    own_values = all_to_all(V)
    outer_first(2, K)
    z_parts_done(K)
    outer_first(3, K)
    outer_second(2, K)
    outer_second(3, K)
    outer_done(K)
    keys()
    stage_keys = pltpu.make_async_copy(stage.at[1], stage_ref, local_sem.at[6])
    stage_keys.start()
    own_values.wait()
    stage_keys.wait()
    for d in range(3):
        arrived(("a2a", V, d))
    for d in (1, 2, 3):
        arrived(("across", d))
    arrived(("ahead", 2), ("behind", 2))
    for copy in copies.values():
        copy.wait_send()


N_COPIES = 4 + 4 * 24 + 2 * 12 + 4 * 12 + 1 + 10


ATTEND_ROWS = GROUP * 3 * 8


def attend(side, q_ref, keys_ref, values_ref, fresh_ref, page_at, length, weight):
    factor = 1.0 / math.sqrt(HEAD)
    steps = 3
    lane = lax.broadcasted_iota(jnp.int32, (1, LANES), 1)
    r = lax.broadcasted_iota(jnp.int32, (ATTEND_ROWS, steps * 8), 0)
    c = lax.broadcasted_iota(jnp.int32, (ATTEND_ROWS, steps * 8), 1)
    visible = (jnp.bitwise_and(r, 7) == jnp.bitwise_and(c, 7)) & (
        jnp.right_shift(lax.rem(r, steps * 8), 3) >= jnp.right_shift(c, 3)
    )
    samples = slice(side * 8, side * 8 + 8)
    query = jnp.concatenate(
        [
            q_ref[:, samples, g * HEAD : (g + 1) * HEAD].astype(F32).reshape(steps * 8, HEAD)
            for g in range(GROUP)
        ],
        axis=0,
    ).astype(BF16)
    new = [
        fresh_ref[kind]
        .astype(F32)
        .reshape(steps, 16, HEAD)[:, samples]
        .reshape(steps * 8, HEAD)
        .astype(BF16)
        for kind in range(2)
    ]
    sums = jnp.zeros((ATTEND_ROWS, LANES), F32)
    for page in range(16):
        chip, part = page // 4, page % 4
        keys = keys_ref[chip, part * PAGE : (part + 1) * PAGE]
        scale = keys_ref[chip, CHIP_TOKENS : CHIP_TOKENS + 16].astype(F32)[part : part + 1]
        raw = lax.dot_general(query, keys, (((1,), (1,)), ((), ())), preferred_element_type=F32)
        live = page_at(page) * PAGE + lane < length
        cached = jnp.where(live, jnp.exp(raw * scale * factor), 0.0)
        weight[:, page * PAGE : (page + 1) * PAGE] = cached
        sums += cached
    fresh_raw = lax.dot_general(
        query, new[0], (((1,), (1,)), ((), ())), preferred_element_type=F32
    )
    fresh = jnp.where(visible, jnp.exp(fresh_raw * factor), 0.0)
    total = jnp.sum(sums, axis=1, keepdims=True) + jnp.sum(fresh, axis=1, keepdims=True)
    result = jnp.dot((fresh / total).astype(BF16), new[1], preferred_element_type=F32)
    for page in range(16):
        chip, part = page // 4, page % 4
        scale = values_ref[chip, CHIP_TOKENS : CHIP_TOKENS + 16].astype(F32)[part : part + 1]
        portion = weight[:, page * PAGE : (page + 1) * PAGE] / total * scale
        result += jnp.dot(
            portion.astype(BF16),
            values_ref[chip, part * PAGE : (part + 1) * PAGE],
            preferred_element_type=F32,
        )
    return [
        result[g * steps * 8 : (g + 1) * steps * 8].reshape(steps, 8, HEAD) for g in range(GROUP)
    ]


def exchange(
    mask, pool_ref, across_ref, stage_ref, far_ref, keys_ref, send_sem, recv_sem, local_sem
):
    dp = lax.axis_index("dp")
    seq = lax.axis_index("seq")
    core = lax.rem(seq, 2)
    z_lo = seq // 2
    partner = jnp.bitwise_xor(dp, mask)
    far_chips = [jnp.bitwise_xor(z_lo, d) for d in (1, 2, 3)]
    columns = [(dp, chip * 2 + core) for chip in far_chips]
    partners = [(partner, jnp.bitwise_xor(z_lo, d) * 2 + core) for d in range(4)]
    plane = mask & ~4
    held = across_ref if mask & 4 else pool_ref
    holder = (jnp.bitwise_xor(dp, plane), seq)

    peers = columns + partners
    if plane and mask & 4:
        peers = peers + [holder]
    barrier = pltpu.get_barrier_semaphore()
    for peer in peers:
        pl.semaphore_signal(barrier, inc=1, device_id=peer, device_id_type=MESH)
    own = pltpu.make_async_copy(stage_ref.at[z_lo], keys_ref.at[z_lo], local_sem.at[0])
    own.start()
    pl.semaphore_wait(barrier, len(peers))

    copies = []

    def send(src, dst, device):
        k = len(copies)
        copy = pltpu.make_async_remote_copy(
            src_ref=src,
            dst_ref=dst,
            send_sem=send_sem.at[k],
            recv_sem=recv_sem.at[k],
            device_id=device,
            device_id_type=MESH,
        )
        copy.start()
        copies.append(copy)

    for d in range(4):
        send(stage_ref.at[jnp.bitwise_xor(z_lo, d)], far_ref.at[0, z_lo], partners[d])
    if plane:
        send(held, far_ref.at[1], holder)
    else:
        local = pltpu.make_async_copy(held, far_ref.at[1], local_sem.at[1])
        local.start()
        local.wait()
    for d in (1, 2, 3):
        send(stage_ref.at[far_chips[d - 1]], keys_ref.at[z_lo], columns[d - 1])
    own.wait()
    for copy in copies:
        copy.wait()


def finish(
    q_ref,
    table_ref,
    length_ref,
    source_ref,
    keys_ref,
    values_ref,
    far_ref,
    fresh_ref,
    out_ref,
    fork_ref,
    weight,
):
    dp = lax.axis_index("dp")
    partner = source_ref[dp]
    near = attend(
        0,
        q_ref,
        keys_ref,
        values_ref,
        fresh_ref,
        lambda page: table_ref[page, dp],
        length_ref[dp],
        weight,
    )
    far = attend(
        1,
        q_ref,
        far_ref.at[0],
        far_ref.at[1],
        fresh_ref,
        lambda page: table_ref[page, partner],
        length_ref[partner],
        weight,
    )
    for g in range(GROUP):
        span = slice(g * HEAD, (g + 1) * HEAD)
        out_ref[:, :, span] = jnp.concatenate([near[g], far[g]], axis=1).astype(BF16)
    for kind in range(2):
        for page in range(16):
            chip, part = page // 4, page % 4
            scale = far_ref[kind, chip, CHIP_TOKENS : CHIP_TOKENS + 16].astype(F32)[
                part : part + 1
            ]
            fork_ref[0, kind, page * PAGE : (page + 1) * PAGE] = (
                far_ref[kind, chip, part * PAGE : (part + 1) * PAGE].astype(F32) * scale
            )


def on_device(
    prompt_hidden,
    key_value_weight,
    key_norm_gain,
    page_table,
    lengths,
    source_replica,
    decode_hidden,
    queries,
):
    steps, paired, width = queries.shape
    replicas = lax.axis_size("dp")
    table = page_table.T
    freq = 500000.0 ** (-np.arange(HEAD // 2) * 2.0 / HEAD)
    freq = jnp.asarray(np.concatenate([freq, freq])[None].astype(np.float32))

    vmem = pl.BlockSpec(memory_space=pltpu.VMEM)
    smem = pl.BlockSpec(memory_space=pltpu.SMEM)
    hbm = pl.BlockSpec(memory_space=pl.ANY)
    pinned = pl.BlockSpec(memory_space=pltpu.HBM)
    pool, across, stage, fresh = pl.pallas_call(
        gather_project,
        out_shape=(
            jax.ShapeDtypeStruct((4, SLAB, LANES), BF16),
            jax.ShapeDtypeStruct((4, SLAB, LANES), BF16),
            jax.ShapeDtypeStruct((4, SLAB, LANES), BF16),
            jax.ShapeDtypeStruct((2, FRESH, LANES), BF16),
        ),
        in_specs=[pinned] * 8,
        out_specs=(hbm, hbm, hbm, vmem),
        scratch_shapes=[
            pltpu.VMEM((SHARD, 2 * HEADS * HEAD), BF16),
            pltpu.SMEM((16, 32), jnp.int32),
            pltpu.SMEM((32,), jnp.int32),
            pltpu.SMEM((32,), jnp.int32),
            pltpu.VMEM((1, LANES), F32),
            pltpu.VMEM((HEADS, HEAD), F32),
            pltpu.VMEM((2, PADDED, 8 * LANES), BF16),
            pltpu.VMEM((4, PADDED, 8 * LANES), BF16),
            pltpu.VMEM((ROWS, WIDTH), BF16),
            pltpu.VMEM((2, 2, 4, 4, 4, BLOCK, LANES), BF16),
            pltpu.VMEM((2, ROWS, 2 * LANES), F32),
            pltpu.VMEM((2, 4, SLAB, LANES), BF16),
            pltpu.VMEM((2, ROWS, LANES), F32),
            pltpu.VMEM((2, ROWS, LANES), F32),
            pltpu.VMEM((2, 272, LANES), BF16),
            pltpu.SemaphoreType.DMA((N_COPIES,)),
            pltpu.SemaphoreType.DMA((N_COPIES,)),
            pltpu.SemaphoreType.DMA((16,)),
        ],
        compiler_params=pltpu.CompilerParams(
            collective_id=0, has_side_effects=True, vmem_limit_bytes=44 * 1024 * 1024
        ),
    )(
        key_value_weight,
        prompt_hidden,
        decode_hidden,
        table,
        lengths,
        source_replica,
        freq,
        key_norm_gain.reshape(HEADS, HEAD),
    )

    def exchange_by(mask):
        return pl.pallas_call(
            functools.partial(exchange, mask),
            out_shape=(
                jax.ShapeDtypeStruct((2, 4, SLAB, LANES), BF16),
                jax.ShapeDtypeStruct((4, SLAB, LANES), BF16),
            ),
            in_specs=[hbm, hbm, hbm],
            out_specs=(hbm, hbm),
            scratch_shapes=[
                pltpu.SemaphoreType.DMA((8,)),
                pltpu.SemaphoreType.DMA((8,)),
                pltpu.SemaphoreType.DMA((2,)),
            ],
            compiler_params=pltpu.CompilerParams(collective_id=mask, has_side_effects=True),
        )

    far_pool, near_keys = lax.switch(
        source_replica[0] - 1,
        [exchange_by(mask) for mask in range(1, replicas)],
        pool,
        across,
        stage,
    )

    attended, forked = pl.pallas_call(
        finish,
        out_shape=(
            jax.ShapeDtypeStruct((steps, paired, width), BF16),
            jax.ShapeDtypeStruct((1, 2, 2048, LANES), F32),
        ),
        in_specs=[vmem, smem, smem, smem, vmem, vmem, vmem, vmem],
        out_specs=(vmem, vmem),
        scratch_shapes=[pltpu.VMEM((ATTEND_ROWS, 2048), F32)],
        compiler_params=pltpu.CompilerParams(vmem_limit_bytes=32 * 1024 * 1024),
    )(queries, table, lengths, source_replica, near_keys, pool, far_pool, fresh)
    return attended, forked


def solution(mesh):
    return jax.shard_map(
        on_device,
        mesh=mesh,
        in_specs=(
            P("dp", "seq", None),
            P(("dp", "seq"), None),
            P(),
            P(),
            P(),
            P(),
            P(None, "dp", None),
            P(None, "dp", "seq"),
        ),
        out_specs=(P(None, "dp", "seq"), P("dp", None, None, "seq")),
        check_vma=False,
    )
```

```python
import functools
import math

import jax
import jax.numpy as jnp
import numpy as np
from jax import lax
from jax.experimental import pallas as pl
from jax.experimental.pallas import tpu as pltpu
from jax.sharding import PartitionSpec as P

HEADS = 8
HEAD = 128
PAGE = 128
GROUP = 5
MESH = pl.DeviceIdType.MESH
F32 = jnp.float32
BF16 = jnp.bfloat16

WIDTH = 5120
SHARD = 20
PADDED = 32
PAIR_ROWS = 80
BLOCK = 160
TOKENS = 256
CHIP_TOKENS = 512
FRESH = 48
ROWS = CHIP_TOKENS + FRESH
SLAB = CHIP_TOKENS + 16
LANES = 128
UPPER = pl.ds(0, 272)
LOWER = pl.ds(272, 256)


def trig(angle):
    lane = lax.broadcasted_iota(jnp.int32, angle.shape, 1)
    return jnp.cos(angle), jnp.where(lane < HEAD // 2, -jnp.sin(angle), jnp.sin(angle))


def gather_project(
    w_hbm,
    prompt_ref,
    decode_ref,
    table_hbm,
    length_hbm,
    source_hbm,
    freq_hbm,
    gain_hbm,
    pool_ref,
    across_ref,
    stage_ref,
    fresh_ref,
    w_ref,
    table_ref,
    length_ref,
    source_ref,
    freq_ref,
    gain_ref,
    split,
    raw,
    acts,
    weights,
    acc,
    stage,
    squares,
    turns,
    relay,
    send_sem,
    recv_sem,
    local_sem,
):
    dp = lax.axis_index("dp")
    seq = lax.axis_index("seq")
    core = lax.rem(seq, 2)
    z_lo = seq // 2
    x = lax.rem(dp, 4)
    z_hi = lax.rem(dp // 4, 2)
    y = dp // 8
    z = z_hi * 4 + z_lo
    pair = z // 2
    odd = lax.rem(z, 2)

    def at(yy, zz, xx, cc):
        return (yy * 8 + (zz // 4) * 4 + xx, lax.rem(zz, 4) * 2 + cc)

    def turn(index, by, size):
        return lax.rem(index + (by + size), size)

    sibling = at(y, z, x, 1 - core)
    inter_z = turn(z, 2 * odd - 1, 8)
    intra_z = z + 1 - 2 * odd
    inter = at(y, inter_z, x, core)
    intra = at(y, intra_z, x, core)
    intra_other = at(y, intra_z, x, 1 - core)
    rights = {"x": at(y, z, turn(x, 1, 4), core), "y": at(turn(y, 1, 4), z, x, core)}
    lefts = {"x": at(y, z, turn(x, -1, 4), core), "y": at(turn(y, -1, 4), z, x, core)}
    far_chips = [jnp.bitwise_xor(z_lo, d) for d in (1, 2, 3)]
    columns = [(dp, chip * 2 + core) for chip in far_chips]
    opposite = [
        (jnp.bitwise_xor(dp, 4), jnp.bitwise_xor(z_lo, d) * 2 + core) for d in range(4)
    ]

    ahead = at(y, turn(z, 2, 8), x, core)
    behind = at(y, turn(z, -2, 8), x, core)

    peers = opposite[1:] + [
        ahead,
        behind,
        sibling,
        inter,
        intra,
        intra_other,
        rights["x"],
        lefts["x"],
        rights["y"],
        lefts["y"],
        columns[1],
        columns[2],
    ]
    barrier = pltpu.get_barrier_semaphore()
    for peer in peers:
        pl.semaphore_signal(barrier, inc=1, device_id=peer, device_id_type=MESH)

    small = [
        pltpu.make_async_copy(src, dst, local_sem.at[8 + k])
        for k, (src, dst) in enumerate(
            [
                (w_hbm, w_ref),
                (table_hbm, table_ref),
                (length_hbm, length_ref),
                (source_hbm, source_ref),
                (freq_hbm, freq_ref),
                (gain_hbm, gain_ref),
            ]
        )
    ]
    for copy in small:
        copy.start()
    own_acts = pltpu.make_async_copy(
        prompt_ref.at[0],
        acts.at[pl.ds(pl.multiple_of(core * TOKENS, TOKENS), TOKENS)],
        local_sem.at[0],
    )
    own_acts.start()
    own_decode = [
        pltpu.make_async_copy(
            decode_ref.at[step], acts.at[pl.ds(CHIP_TOKENS + step * 16, 16)], local_sem.at[1 + step]
        )
        for step in range(3)
    ]
    for copy in own_decode:
        copy.start()

    small[0].wait()
    keep = jnp.where(
        lax.broadcasted_iota(jnp.int32, (PADDED, SHARD), 0)
        == lax.broadcasted_iota(jnp.int32, (PADDED, SHARD), 1),
        1.0,
        0.0,
    ).astype(BF16)
    for g in range(2):
        for c in range(2):
            tiles = [
                w_ref[:, pl.ds((1 - g) * HEADS * HEAD + (2 * i + c) * HEAD, HEAD)] for i in range(4)
            ]
            split[g, c] = jnp.dot(
                keep, jnp.concatenate(tiles, axis=1), preferred_element_type=F32
            ).astype(BF16)
        raw[g, odd * 2 + core] = split[g, core]
    pl.semaphore_wait(barrier, len(peers))

    number = [0]
    copies = {}

    def send(key, src, dst, device):
        k = number[0]
        number[0] += 1
        copy = pltpu.make_async_remote_copy(
            src_ref=src,
            dst_ref=dst,
            send_sem=send_sem.at[k],
            recv_sem=recv_sem.at[k],
            device_id=device,
            device_id_type=MESH,
        )
        copy.start()
        copies[key] = copy

    def arrived(*keys):
        for key in keys:
            copies[key].wait_recv()

    slot = odd * 2 + core
    for g in range(2):
        send(("w_intra", g), split.at[g, core], raw.at[g, slot], intra)
        send(("w_other", g), split.at[g, 1 - core], raw.at[g, slot], intra_other)
        send(("w_sibling", g), split.at[g, 1 - core], raw.at[g, slot], sibling)

    here = pl.ds(pl.multiple_of(core * TOKENS, TOKENS), TOKENS)
    send("acts", prompt_ref.at[0], acts.at[here], sibling)

    row = lax.broadcasted_iota(jnp.int32, (PAIR_ROWS, 4 * PADDED), 0)
    col = lax.broadcasted_iota(jnp.int32, (PAIR_ROWS, 4 * PADDED), 1)
    inside = jnp.bitwise_and(col, PADDED - 1)
    source = jnp.right_shift(col, 5)
    pick = jnp.where((row == source * SHARD + inside) & (inside < SHARD), 1.0, 0.0).astype(BF16)

    outer = (y, x)
    inner = (x, y)
    inner_axis = ("x", "y")
    outer_axis = ("y", "x")

    def assemble(g):
        arrived(("w_intra", g), ("w_other", g), ("w_sibling", g))
        rows = jnp.dot(
            pick, raw[g].reshape(4 * PADDED, 4 * LANES), preferred_element_type=F32
        ).astype(BF16)
        for p in range(2):
            for t in range(2):
                tile = p * 2 + t
                weights[g, p, outer[p], pair, inner[p], pl.ds(t * PAIR_ROWS, PAIR_ROWS)] = rows[
                    :, tile * LANES : (tile + 1) * LANES
                ]

    offsets = (0, -1, 1, 2)
    sign = 2 * odd - 1
    blocks = [pair, turn(pair, sign, 4), turn(pair, -sign, 4), turn(pair, 2, 4)]

    def inner_first(g):
        for p in range(2):
            ref = weights.at[g, p, outer[p], pair, inner[p]]
            send(("i1r", g, p), ref, ref, rights[inner_axis[p]])
            send(("i1l", g, p), ref, ref, lefts[inner_axis[p]])

    def inner_second(g):
        for p in range(2):
            arrived(("i1r", g, p), ("i1l", g, p))
            ref = weights.at[g, p, outer[p], pair]
            low = ref.at[turn(inner[p], -1, 4), pl.ds(0, PAIR_ROWS)]
            high = ref.at[turn(inner[p], 1, 4), pl.ds(PAIR_ROWS, PAIR_ROWS)]
            send(("i2r", g, p), low, low, rights[inner_axis[p]])
            send(("i2l", g, p), high, high, lefts[inner_axis[p]])

    def inner_done(g):
        for p in range(2):
            arrived(("i2r", g, p), ("i2l", g, p))

    def z_step(step, g):
        half = (1 - odd) if step == 3 else odd
        for p in range(2):
            if step >= 2:
                arrived(("z", step - 1, g, p))
            ref = weights.at[g, p, outer[p], blocks[step - 1]]
            if step >= 3:
                ref = ref.at[pl.ds(half * 2, 2)]
            send(("z", step, g, p), ref, ref, inter if step % 2 else intra)

    def z_part(step, part, g):
        half = (1 - odd) if step == 3 else odd
        for p in range(2):
            at_part = turn(inner[p], offsets[part], 4)
            if step >= 2:
                arrived(("zp", step - 1, part, g, p))
            ref = weights.at[g, p, outer[p], blocks[step - 1], at_part]
            if step >= 3:
                ref = ref.at[pl.ds(pl.multiple_of(half * PAIR_ROWS, 16), PAIR_ROWS)]
            send(("zp", step, part, g, p), ref, ref, inter if step % 2 else intra)

    def z_parts_done(g):
        for part in range(4):
            for p in range(2):
                arrived(("zp", 4, part, g, p))

    def z_done(g):
        for p in range(2):
            arrived(("z", 4, g, p))

    def outer_first(block, g):
        for p in range(2):
            ref = weights.at[g, p, outer[p], blocks[block]]
            send(("o1r", block, g, p), ref, ref, rights[outer_axis[p]])
            send(("o1l", block, g, p), ref, ref, lefts[outer_axis[p]])

    def outer_second(block, g):
        for p in range(2):
            arrived(("o1r", block, g, p), ("o1l", block, g, p))
            low = weights.at[g, p, turn(outer[p], -1, 4), blocks[block], pl.ds(0, 2)]
            high = weights.at[g, p, turn(outer[p], 1, 4), blocks[block], pl.ds(2, 2)]
            send(("o2r", block, g, p), low, low, rights[outer_axis[p]])
            send(("o2l", block, g, p), high, high, lefts[outer_axis[p]])

    def own_first(part, g):
        for p in range(2):
            ref = weights.at[g, p, outer[p], pair, turn(inner[p], offsets[part], 4)]
            send(("q1r", part, g, p), ref, ref, rights[outer_axis[p]])
            send(("q1l", part, g, p), ref, ref, lefts[outer_axis[p]])

    def own_second(part, g):
        for p in range(2):
            arrived(("q1r", part, g, p), ("q1l", part, g, p))
            at_part = turn(inner[p], offsets[part], 4)
            low = weights.at[g, p, turn(outer[p], -1, 4), pair, at_part, pl.ds(0, PAIR_ROWS)]
            high = weights.at[
                g, p, turn(outer[p], 1, 4), pair, at_part, pl.ds(PAIR_ROWS, PAIR_ROWS)
            ]
            send(("q2r", part, g, p), low, low, rights[outer_axis[p]])
            send(("q2l", part, g, p), high, high, lefts[outer_axis[p]])

    def outer_done(g):
        for p in range(2):
            if g == 0:
                for part in range(4):
                    arrived(("q2r", part, g, p), ("q2l", part, g, p))
            for block in range(1 - g, 4):
                arrived(("o2r", block, g, p), ("o2l", block, g, p))

    def add(g, p, yy, fresh=False):
        tiles = []
        for t in range(2):
            pieces = []
            for zh in range(2):
                for xx in range(4):
                    for zl in range(2):
                        place = (yy, xx) if p == 0 else (xx, yy)
                        pieces.append(
                            weights[
                                g,
                                p,
                                place[0],
                                zh * 2 + zl,
                                place[1],
                                pl.ds(t * PAIR_ROWS, PAIR_ROWS),
                            ]
                        )
            tiles.append(jnp.concatenate(pieces, axis=0))
        product = jnp.dot(
            acts[:, pl.ds(pl.multiple_of(yy * 1280, 1280), 1280)],
            jnp.concatenate(tiles, axis=1),
            preferred_element_type=F32,
        )
        acc[p] = product if fresh else acc[p] + product

    def project_early(g):
        add(g, 0, y, True)

        @pl.loop(0, 2)
        def _(k):
            add(g, 0, lax.rem(y + 1 + 2 * k, 4))

    def project(g):
        add(g, 0, turn(y, 2, 4))
        add(g, 1, 0, True)

        @pl.loop(1, 4)
        def _(yy):
            add(g, 1, yy)

    def pack(g):
        peaks = []
        for head in range(4):
            p, lanes = head // 2, pl.ds(head % 2 * LANES, LANES)
            for page in range(4):
                part = pl.ds(page * PAGE, PAGE)
                peaks.append(jnp.max(jnp.abs(acc[p, part, lanes]), axis=0, keepdims=True))
        largest = jnp.max(jnp.concatenate(peaks, axis=0), axis=1, keepdims=True)
        scale = ((largest + 1e-06) / 448.0).astype(BF16).astype(F32)
        inverse = 1.0 / scale
        row = lax.broadcasted_iota(jnp.int32, (16, LANES), 0)
        for head in range(4):
            p, lanes = head // 2, pl.ds(head % 2 * LANES, LANES)
            rows = jnp.zeros((16, LANES), F32)
            for page in range(4):
                part = pl.ds(page * PAGE, PAGE)
                k = head * 4 + page
                stage[g, head, part] = (acc[p, part, lanes] * inverse[k : k + 1]).astype(BF16)
                rows = jnp.where(row == page, scale[k : k + 1], rows)
            stage[g, head, pl.ds(CHIP_TOKENS, 16)] = rows.astype(BF16)

    def all_to_all(g):
        for d in range(3):
            send(
                ("a2a", g, d), stage.at[g, far_chips[d]], pool_ref.at[z_lo], columns[d]
            )
        send(("ahead", 1), stage.at[g, z_lo, UPPER], relay.at[0, UPPER], ahead)
        send(("behind", 1), stage.at[g, z_lo, LOWER], relay.at[1, pl.ds(0, 256)], behind)
        for d in (1, 2, 3):
            send(
                ("across", d),
                stage.at[g, jnp.bitwise_xor(z_lo, d)],
                across_ref.at[z_lo],
                opposite[d],
            )
        own = pltpu.make_async_copy(stage.at[g, z_lo], pool_ref.at[z_lo], local_sem.at[4])
        own.start()
        return own

    def pass_on():
        arrived(("ahead", 1), ("behind", 1))
        place = jnp.bitwise_xor(z_lo, 2)
        send(("ahead", 2), relay.at[0, UPPER], across_ref.at[place, UPPER], ahead)
        send(("behind", 2), relay.at[1, pl.ds(0, 256)], across_ref.at[place, LOWER], behind)

    line = lax.broadcasted_iota(jnp.int32, (PAGE, LANES), 0)
    def first(page):
        return table_ref[z_lo * 4 + page, dp] * PAGE

    def live(page):
        return first(page) + line < length_ref[dp]

    def angles():
        for copy in small[1:]:
            copy.wait()
        for page in range(4):
            angle = (first(page) + line).astype(F32) * freq_ref[...]
            part = pl.ds(page * PAGE, PAGE)
            turns[0, part], turns[1, part] = trig(angle)
        row = lax.broadcasted_iota(jnp.int32, (FRESH, LANES), 0)
        far_length = length_ref[source_ref[dp]]
        start = jnp.where(jnp.bitwise_and(row, 15) < 8, length_ref[dp], far_length)
        angle = (start + jnp.right_shift(row, 4)).astype(F32) * freq_ref[...]
        part = pl.ds(CHIP_TOKENS, FRESH)
        turns[0, part], turns[1, part] = trig(angle)

    tail = pl.ds(CHIP_TOKENS, FRESH)

    def keep_fresh(kind):
        for head in range(4):
            p, lanes = head // 2, pl.ds(head % 2 * LANES, LANES)

            @pl.when(z_lo == head)
            def _():
                fresh_ref[kind] = acc[p, tail, lanes].astype(BF16)

    def values():
        project(0)
        keep_fresh(1)
        for page in range(4):
            part = pl.ds(page * PAGE, PAGE)
            for head in range(4):
                p, lanes = head // 2, pl.ds(head % 2 * LANES, LANES)
                acc[p, part, lanes] = jnp.where(live(page), acc[p, part, lanes], 0.0)
        pack(0)

    def keys():
        project(1)
        total = jnp.zeros((ROWS, 1), F32)
        for p in range(2):
            total += jnp.sum(acc[p] * acc[p], axis=1, keepdims=True)
        squares[0] = jnp.broadcast_to(total, (ROWS, LANES))
        send("squares", squares.at[0], squares.at[1], sibling)
        pass_on()
        parts = [pl.ds(page * PAGE, PAGE) for page in range(4)] + [tail]
        for head in range(4):
            p, lanes = head // 2, pl.ds(head % 2 * LANES, LANES)
            gain = gain_ref[pl.ds(head * 2 + core, 1), :]
            for part in parts:
                row = acc[p, part, lanes] * gain
                acc[p, part, lanes] = row * turns[0, part] + pltpu.roll(row, 64, 1) * turns[1, part]
        arrived("squares")
        for page, part in enumerate(parts):
            norm = lax.rsqrt((squares[0, part] + squares[1, part]) * (1.0 / (HEADS * HEAD)) + 1e-06)
            if page < 4:
                norm = jnp.where(live(page), norm, 0.0)
            for head in range(4):
                p, lanes = head // 2, pl.ds(head % 2 * LANES, LANES)
                acc[p, part, lanes] = acc[p, part, lanes] * norm
        keep_fresh(0)
        pack(1)

    V, K = 0, 1
    assemble(V)
    inner_first(V)
    z_part(1, 0, V)
    own_first(0, V)
    assemble(K)
    z_part(1, 0, K)
    inner_first(K)
    inner_second(V)
    z_part(1, 1, V)
    z_part(1, 2, V)
    own_first(1, V)
    own_first(2, V)
    z_part(2, 0, V)
    own_second(0, V)
    inner_done(V)
    z_part(1, 3, V)
    own_first(3, V)
    z_part(2, 0, K)
    own_second(1, V)
    own_second(2, V)
    z_part(3, 0, V)
    z_part(2, 1, V)
    inner_second(K)
    own_second(3, V)
    z_part(2, 2, V)
    z_part(3, 0, K)
    inner_done(K)
    outer_first(0, K)
    z_part(1, 1, K)
    z_part(3, 1, V)
    z_part(2, 3, V)
    outer_first(1, V)
    angles()
    z_part(4, 0, V)
    z_part(3, 2, V)
    z_part(4, 0, K)
    z_part(1, 2, K)
    z_part(3, 3, V)
    outer_first(2, V)
    z_part(2, 1, K)
    z_part(4, 1, V)
    z_part(4, 2, V)
    z_part(1, 3, K)
    z_part(2, 2, K)
    z_part(3, 1, K)
    outer_second(1, V)
    z_part(4, 3, V)
    z_part(2, 3, K)
    z_part(3, 2, K)
    z_part(4, 1, K)
    outer_second(2, V)
    z_parts_done(V)
    outer_first(3, V)
    z_part(4, 2, K)
    z_part(3, 3, K)
    z_part(4, 3, K)
    outer_second(0, K)
    outer_second(3, V)
    outer_first(1, K)
    own_acts.wait()
    for copy in own_decode:
        copy.wait()
    arrived("acts")
    project_early(V)
    outer_done(V)
    values()
    outer_second(1, K)
    own_values = all_to_all(V)
    outer_first(2, K)
    z_parts_done(K)
    outer_first(3, K)
    outer_second(2, K)
    outer_second(3, K)
    project_early(K)
    outer_done(K)
    keys()
    stage_keys = pltpu.make_async_copy(stage.at[1], stage_ref, local_sem.at[6])
    stage_keys.start()
    own_values.wait()
    stage_keys.wait()
    for d in range(3):
        arrived(("a2a", V, d))
    for d in (1, 2, 3):
        arrived(("across", d))
    arrived(("ahead", 2), ("behind", 2))
    for copy in copies.values():
        copy.wait_send()


N_COPIES = 7 + 4 * 24 + 2 * 12 + 4 * 12 + 1 + 10


ATTEND_ROWS = GROUP * 3 * 8


def attend(side, q_ref, keys_ref, values_ref, fresh_ref, page_at, length, weight):
    factor = 1.0 / math.sqrt(HEAD)
    steps = 3
    lane = lax.broadcasted_iota(jnp.int32, (1, LANES), 1)
    r = lax.broadcasted_iota(jnp.int32, (ATTEND_ROWS, steps * 8), 0)
    c = lax.broadcasted_iota(jnp.int32, (ATTEND_ROWS, steps * 8), 1)
    visible = (jnp.bitwise_and(r, 7) == jnp.bitwise_and(c, 7)) & (
        jnp.right_shift(lax.rem(r, steps * 8), 3) >= jnp.right_shift(c, 3)
    )
    samples = slice(side * 8, side * 8 + 8)
    query = jnp.concatenate(
        [
            q_ref[:, samples, g * HEAD : (g + 1) * HEAD].astype(F32).reshape(steps * 8, HEAD)
            for g in range(GROUP)
        ],
        axis=0,
    ).astype(BF16)
    new = [
        fresh_ref[kind]
        .astype(F32)
        .reshape(steps, 16, HEAD)[:, samples]
        .reshape(steps * 8, HEAD)
        .astype(BF16)
        for kind in range(2)
    ]
    sums = jnp.zeros((ATTEND_ROWS, LANES), F32)
    for page in range(16):
        chip, part = page // 4, page % 4
        keys = keys_ref[chip, part * PAGE : (part + 1) * PAGE]
        scale = keys_ref[chip, CHIP_TOKENS : CHIP_TOKENS + 16].astype(F32)[part : part + 1]
        raw = lax.dot_general(query, keys, (((1,), (1,)), ((), ())), preferred_element_type=F32)
        live = page_at(page) * PAGE + lane < length
        cached = jnp.where(live, jnp.exp(raw * scale * factor), 0.0)
        weight[:, page * PAGE : (page + 1) * PAGE] = cached
        sums += cached
    fresh_raw = lax.dot_general(
        query, new[0], (((1,), (1,)), ((), ())), preferred_element_type=F32
    )
    fresh = jnp.where(visible, jnp.exp(fresh_raw * factor), 0.0)
    total = jnp.sum(sums, axis=1, keepdims=True) + jnp.sum(fresh, axis=1, keepdims=True)
    result = jnp.dot((fresh / total).astype(BF16), new[1], preferred_element_type=F32)
    for page in range(16):
        chip, part = page // 4, page % 4
        scale = values_ref[chip, CHIP_TOKENS : CHIP_TOKENS + 16].astype(F32)[part : part + 1]
        portion = weight[:, page * PAGE : (page + 1) * PAGE] / total * scale
        result += jnp.dot(
            portion.astype(BF16),
            values_ref[chip, part * PAGE : (part + 1) * PAGE],
            preferred_element_type=F32,
        )
    return [
        result[g * steps * 8 : (g + 1) * steps * 8].reshape(steps, 8, HEAD) for g in range(GROUP)
    ]


def exchange(
    mask, pool_ref, across_ref, stage_ref, far_ref, keys_ref, send_sem, recv_sem, local_sem
):
    dp = lax.axis_index("dp")
    seq = lax.axis_index("seq")
    core = lax.rem(seq, 2)
    z_lo = seq // 2
    partner = jnp.bitwise_xor(dp, mask)
    far_chips = [jnp.bitwise_xor(z_lo, d) for d in (1, 2, 3)]
    columns = [(dp, chip * 2 + core) for chip in far_chips]
    partners = [(partner, jnp.bitwise_xor(z_lo, d) * 2 + core) for d in range(4)]
    plane = mask & ~4
    held = across_ref if mask & 4 else pool_ref
    holder = (jnp.bitwise_xor(dp, plane), seq)

    peers = columns + partners
    if plane and mask & 4:
        peers = peers + [holder]
    barrier = pltpu.get_barrier_semaphore()
    for peer in peers:
        pl.semaphore_signal(barrier, inc=1, device_id=peer, device_id_type=MESH)
    own = pltpu.make_async_copy(stage_ref.at[z_lo], keys_ref.at[z_lo], local_sem.at[0])
    own.start()
    pl.semaphore_wait(barrier, len(peers))

    copies = []

    def send(src, dst, device):
        k = len(copies)
        copy = pltpu.make_async_remote_copy(
            src_ref=src,
            dst_ref=dst,
            send_sem=send_sem.at[k],
            recv_sem=recv_sem.at[k],
            device_id=device,
            device_id_type=MESH,
        )
        copy.start()
        copies.append(copy)

    if plane:
        send(held, far_ref.at[1], holder)
    else:
        local = pltpu.make_async_copy(held, far_ref.at[1], local_sem.at[1])
        local.start()
        local.wait()
    for d in (1, 2, 3):
        send(stage_ref.at[far_chips[d - 1]], keys_ref.at[z_lo], columns[d - 1])
    for d in (3, 2, 1, 0):
        send(stage_ref.at[jnp.bitwise_xor(z_lo, d)], far_ref.at[0, z_lo], partners[d])
    own.wait()
    for copy in copies:
        copy.wait()


def finish(
    q_ref,
    table_ref,
    length_ref,
    source_ref,
    keys_ref,
    values_ref,
    far_ref,
    fresh_ref,
    out_ref,
    fork_ref,
    weight,
):
    dp = lax.axis_index("dp")
    partner = source_ref[dp]
    near = attend(
        0,
        q_ref,
        keys_ref,
        values_ref,
        fresh_ref,
        lambda page: table_ref[page, dp],
        length_ref[dp],
        weight,
    )
    far = attend(
        1,
        q_ref,
        far_ref.at[0],
        far_ref.at[1],
        fresh_ref,
        lambda page: table_ref[page, partner],
        length_ref[partner],
        weight,
    )
    for g in range(GROUP):
        span = slice(g * HEAD, (g + 1) * HEAD)
        out_ref[:, :, span] = jnp.concatenate([near[g], far[g]], axis=1).astype(BF16)
    for kind in range(2):
        for page in range(16):
            chip, part = page // 4, page % 4
            scale = far_ref[kind, chip, CHIP_TOKENS : CHIP_TOKENS + 16].astype(F32)[
                part : part + 1
            ]
            fork_ref[0, kind, page * PAGE : (page + 1) * PAGE] = (
                far_ref[kind, chip, part * PAGE : (part + 1) * PAGE].astype(F32) * scale
            )


def on_device(
    prompt_hidden,
    key_value_weight,
    key_norm_gain,
    page_table,
    lengths,
    source_replica,
    decode_hidden,
    queries,
):
    steps, paired, width = queries.shape
    replicas = lax.axis_size("dp")
    table = page_table.T
    freq = 500000.0 ** (-np.arange(HEAD // 2) * 2.0 / HEAD)
    freq = jnp.asarray(np.concatenate([freq, freq])[None].astype(np.float32))

    vmem = pl.BlockSpec(memory_space=pltpu.VMEM)
    smem = pl.BlockSpec(memory_space=pltpu.SMEM)
    hbm = pl.BlockSpec(memory_space=pl.ANY)
    pinned = pl.BlockSpec(memory_space=pltpu.HBM)
    pool, across, stage, fresh = pl.pallas_call(
        gather_project,
        out_shape=(
            jax.ShapeDtypeStruct((4, SLAB, LANES), BF16),
            jax.ShapeDtypeStruct((4, SLAB, LANES), BF16),
            jax.ShapeDtypeStruct((4, SLAB, LANES), BF16),
            jax.ShapeDtypeStruct((2, FRESH, LANES), BF16),
        ),
        in_specs=[pinned] * 8,
        out_specs=(hbm, hbm, hbm, vmem),
        scratch_shapes=[
            pltpu.VMEM((SHARD, 2 * HEADS * HEAD), BF16),
            pltpu.SMEM((16, 32), jnp.int32),
            pltpu.SMEM((32,), jnp.int32),
            pltpu.SMEM((32,), jnp.int32),
            pltpu.VMEM((1, LANES), F32),
            pltpu.VMEM((HEADS, HEAD), F32),
            pltpu.VMEM((2, 2, PADDED, 4 * LANES), BF16),
            pltpu.VMEM((2, 4, PADDED, 4 * LANES), BF16),
            pltpu.VMEM((ROWS, WIDTH), BF16),
            pltpu.VMEM((2, 2, 4, 4, 4, BLOCK, LANES), BF16),
            pltpu.VMEM((2, ROWS, 2 * LANES), F32),
            pltpu.VMEM((2, 4, SLAB, LANES), BF16),
            pltpu.VMEM((2, ROWS, LANES), F32),
            pltpu.VMEM((2, ROWS, LANES), F32),
            pltpu.VMEM((2, 272, LANES), BF16),
            pltpu.SemaphoreType.DMA((N_COPIES,)),
            pltpu.SemaphoreType.DMA((N_COPIES,)),
            pltpu.SemaphoreType.DMA((16,)),
        ],
        compiler_params=pltpu.CompilerParams(
            collective_id=0, has_side_effects=True, vmem_limit_bytes=60 * 1024 * 1024
        ),
    )(
        key_value_weight,
        prompt_hidden,
        decode_hidden,
        table,
        lengths,
        source_replica,
        freq,
        key_norm_gain.reshape(HEADS, HEAD),
    )

    def exchange_by(mask):
        return pl.pallas_call(
            functools.partial(exchange, mask),
            out_shape=(
                jax.ShapeDtypeStruct((2, 4, SLAB, LANES), BF16),
                jax.ShapeDtypeStruct((4, SLAB, LANES), BF16),
            ),
            in_specs=[hbm, hbm, hbm],
            out_specs=(hbm, hbm),
            scratch_shapes=[
                pltpu.SemaphoreType.DMA((8,)),
                pltpu.SemaphoreType.DMA((8,)),
                pltpu.SemaphoreType.DMA((2,)),
            ],
            compiler_params=pltpu.CompilerParams(collective_id=mask, has_side_effects=True),
        )

    far_pool, near_keys = lax.switch(
        source_replica[0] - 1,
        [exchange_by(mask) for mask in range(1, replicas)],
        pool,
        across,
        stage,
    )

    attended, forked = pl.pallas_call(
        finish,
        out_shape=(
            jax.ShapeDtypeStruct((steps, paired, width), BF16),
            jax.ShapeDtypeStruct((1, 2, 2048, LANES), F32),
        ),
        in_specs=[vmem, smem, smem, smem, vmem, vmem, vmem, vmem],
        out_specs=(vmem, vmem),
        scratch_shapes=[pltpu.VMEM((ATTEND_ROWS, 2048), F32)],
        compiler_params=pltpu.CompilerParams(vmem_limit_bytes=32 * 1024 * 1024),
    )(queries, table, lengths, source_replica, near_keys, pool, far_pool, fresh)
    return attended, forked


def solution(mesh):
    return jax.shard_map(
        on_device,
        mesh=mesh,
        in_specs=(
            P("dp", "seq", None),
            P(("dp", "seq"), None),
            P(),
            P(),
            P(),
            P(),
            P(None, "dp", None),
            P(None, "dp", "seq"),
        ),
        out_specs=(P(None, "dp", "seq"), P("dp", None, None, "seq")),
        check_vma=False,
    )
```

```python
import functools
import math

import jax
import jax.numpy as jnp
import numpy as np
from jax import lax
from jax.experimental import pallas as pl
from jax.experimental.pallas import tpu as pltpu
from jax.sharding import PartitionSpec as P

HEADS = 8
HEAD = 128
PAGE = 128
GROUP = 5
MESH = pl.DeviceIdType.MESH
F32 = jnp.float32
BF16 = jnp.bfloat16

WIDTH = 5120
SHARD = 20
PADDED = 32
PAIR_ROWS = 80
BLOCK = 160
TOKENS = 256
CHIP_TOKENS = 512
FRESH = 48
ROWS = CHIP_TOKENS + FRESH
SLAB = CHIP_TOKENS + 16
LANES = 128
UPPER = pl.ds(0, 272)
LOWER = pl.ds(272, 256)


def trig(angle):
    lane = lax.broadcasted_iota(jnp.int32, angle.shape, 1)
    return jnp.cos(angle), jnp.where(lane < HEAD // 2, -jnp.sin(angle), jnp.sin(angle))


def gather_project(
    w_hbm,
    prompt_ref,
    decode_ref,
    table_hbm,
    length_hbm,
    source_hbm,
    freq_hbm,
    gain_hbm,
    pool_ref,
    across_ref,
    stage_ref,
    fresh_ref,
    w_ref,
    table_ref,
    length_ref,
    source_ref,
    freq_ref,
    gain_ref,
    split,
    raw,
    acts,
    acts_x,
    weights,
    acc,
    stage,
    squares,
    turns,
    relay,
    send_sem,
    recv_sem,
    local_sem,
):
    dp = lax.axis_index("dp")
    seq = lax.axis_index("seq")
    core = lax.rem(seq, 2)
    z_lo = seq // 2
    x = lax.rem(dp, 4)
    z_hi = lax.rem(dp // 4, 2)
    y = dp // 8
    z = z_hi * 4 + z_lo
    pair = z // 2
    odd = lax.rem(z, 2)

    def at(yy, zz, xx, cc):
        return (yy * 8 + (zz // 4) * 4 + xx, lax.rem(zz, 4) * 2 + cc)

    def turn(index, by, size):
        return lax.rem(index + (by + size), size)

    sibling = at(y, z, x, 1 - core)
    inter_z = turn(z, 2 * odd - 1, 8)
    intra_z = z + 1 - 2 * odd
    inter = at(y, inter_z, x, core)
    intra = at(y, intra_z, x, core)
    intra_other = at(y, intra_z, x, 1 - core)
    rights = {"x": at(y, z, turn(x, 1, 4), core), "y": at(turn(y, 1, 4), z, x, core)}
    lefts = {"x": at(y, z, turn(x, -1, 4), core), "y": at(turn(y, -1, 4), z, x, core)}
    far_chips = [jnp.bitwise_xor(z_lo, d) for d in (1, 2, 3)]
    columns = [(dp, chip * 2 + core) for chip in far_chips]
    opposite = [
        (jnp.bitwise_xor(dp, 4), jnp.bitwise_xor(z_lo, d) * 2 + core) for d in range(4)
    ]

    ahead = at(y, turn(z, 2, 8), x, core)
    behind = at(y, turn(z, -2, 8), x, core)

    peers = opposite[1:] + [
        ahead,
        behind,
        sibling,
        inter,
        intra,
        intra_other,
        rights["x"],
        lefts["x"],
        rights["y"],
        lefts["y"],
        columns[1],
        columns[2],
    ]
    barrier = pltpu.get_barrier_semaphore()
    for peer in peers:
        pl.semaphore_signal(barrier, inc=1, device_id=peer, device_id_type=MESH)

    small = [
        pltpu.make_async_copy(src, dst, local_sem.at[8 + k])
        for k, (src, dst) in enumerate(
            [
                (w_hbm, w_ref),
                (table_hbm, table_ref),
                (length_hbm, length_ref),
                (source_hbm, source_ref),
                (freq_hbm, freq_ref),
                (gain_hbm, gain_ref),
            ]
        )
    ]
    for copy in small:
        copy.start()
    own_acts = pltpu.make_async_copy(
        prompt_ref.at[0],
        acts.at[pl.ds(pl.multiple_of(core * TOKENS, TOKENS), TOKENS)],
        local_sem.at[0],
    )
    own_acts.start()
    own_decode = [
        pltpu.make_async_copy(
            decode_ref.at[step], acts.at[pl.ds(CHIP_TOKENS + step * 16, 16)], local_sem.at[1 + step]
        )
        for step in range(3)
    ]
    for copy in own_decode:
        copy.start()

    small[0].wait()
    keep = jnp.where(
        lax.broadcasted_iota(jnp.int32, (PADDED, SHARD), 0)
        == lax.broadcasted_iota(jnp.int32, (PADDED, SHARD), 1),
        1.0,
        0.0,
    ).astype(BF16)
    for g in range(2):
        for c in range(2):
            tiles = [
                w_ref[:, pl.ds((1 - g) * HEADS * HEAD + (2 * i + c) * HEAD, HEAD)] for i in range(4)
            ]
            split[g, c] = jnp.dot(
                keep, jnp.concatenate(tiles, axis=1), preferred_element_type=F32
            ).astype(BF16)
        raw[g, odd * 2 + core] = split[g, core]
    pl.semaphore_wait(barrier, len(peers))

    number = [0]
    copies = {}

    def send(key, src, dst, device):
        k = number[0]
        number[0] += 1
        copy = pltpu.make_async_remote_copy(
            src_ref=src,
            dst_ref=dst,
            send_sem=send_sem.at[k],
            recv_sem=recv_sem.at[k],
            device_id=device,
            device_id_type=MESH,
        )
        copy.start()
        copies[key] = copy

    def arrived(*keys):
        for key in keys:
            copies[key].wait_recv()

    slot = odd * 2 + core
    for g in range(2):
        send(("w_intra", g), split.at[g, core], raw.at[g, slot], intra)
        send(("w_other", g), split.at[g, 1 - core], raw.at[g, slot], intra_other)
        send(("w_sibling", g), split.at[g, 1 - core], raw.at[g, slot], sibling)

    here = pl.ds(pl.multiple_of(core * TOKENS, TOKENS), TOKENS)
    send("acts", prompt_ref.at[0], acts.at[here], sibling)

    row = lax.broadcasted_iota(jnp.int32, (PAIR_ROWS, 4 * PADDED), 0)
    col = lax.broadcasted_iota(jnp.int32, (PAIR_ROWS, 4 * PADDED), 1)
    inside = jnp.bitwise_and(col, PADDED - 1)
    source = jnp.right_shift(col, 5)
    pick = jnp.where((row == source * SHARD + inside) & (inside < SHARD), 1.0, 0.0).astype(BF16)

    outer = (y, x)
    inner = (x, y)
    inner_axis = ("x", "y")
    outer_axis = ("y", "x")

    def assemble(g):
        arrived(("w_intra", g), ("w_other", g), ("w_sibling", g))
        rows = jnp.dot(
            pick, raw[g].reshape(4 * PADDED, 4 * LANES), preferred_element_type=F32
        ).astype(BF16)
        for p in range(2):
            for t in range(2):
                tile = p * 2 + t
                weights[g, p, outer[p], pair, inner[p], pl.ds(t * PAIR_ROWS, PAIR_ROWS)] = rows[
                    :, tile * LANES : (tile + 1) * LANES
                ]

    offsets = (0, -1, 1, 2)
    sign = 2 * odd - 1
    blocks = [pair, turn(pair, sign, 4), turn(pair, -sign, 4), turn(pair, 2, 4)]

    def inner_first(g):
        for p in range(2):
            ref = weights.at[g, p, outer[p], pair, inner[p]]
            send(("i1r", g, p), ref, ref, rights[inner_axis[p]])
            send(("i1l", g, p), ref, ref, lefts[inner_axis[p]])

    def inner_second(g):
        for p in range(2):
            arrived(("i1r", g, p), ("i1l", g, p))
            ref = weights.at[g, p, outer[p], pair]
            low = ref.at[turn(inner[p], -1, 4), pl.ds(0, PAIR_ROWS)]
            high = ref.at[turn(inner[p], 1, 4), pl.ds(PAIR_ROWS, PAIR_ROWS)]
            send(("i2r", g, p), low, low, rights[inner_axis[p]])
            send(("i2l", g, p), high, high, lefts[inner_axis[p]])

    def inner_done(g):
        for p in range(2):
            arrived(("i2r", g, p), ("i2l", g, p))

    def z_step(step, g):
        half = (1 - odd) if step == 3 else odd
        for p in range(2):
            if step >= 2:
                arrived(("z", step - 1, g, p))
            ref = weights.at[g, p, outer[p], blocks[step - 1]]
            if step >= 3:
                ref = ref.at[pl.ds(half * 2, 2)]
            send(("z", step, g, p), ref, ref, inter if step % 2 else intra)

    def z_part(step, part, g):
        half = (1 - odd) if step == 3 else odd
        for p in range(2):
            at_part = turn(inner[p], offsets[part], 4)
            if step >= 2:
                arrived(("zp", step - 1, part, g, p))
            ref = weights.at[g, p, outer[p], blocks[step - 1], at_part]
            if step >= 3:
                ref = ref.at[pl.ds(pl.multiple_of(half * PAIR_ROWS, 16), PAIR_ROWS)]
            send(("zp", step, part, g, p), ref, ref, inter if step % 2 else intra)

    def z_parts_done(g):
        for part in range(4):
            for p in range(2):
                arrived(("zp", 4, part, g, p))

    def z_done(g):
        for p in range(2):
            arrived(("z", 4, g, p))

    def outer_first(block, g):
        for p in range(2):
            ref = weights.at[g, p, outer[p], blocks[block]]
            send(("o1r", block, g, p), ref, ref, rights[outer_axis[p]])
            send(("o1l", block, g, p), ref, ref, lefts[outer_axis[p]])

    def outer_second(block, g):
        for p in range(2):
            arrived(("o1r", block, g, p), ("o1l", block, g, p))
            low = weights.at[g, p, turn(outer[p], -1, 4), blocks[block], pl.ds(0, 2)]
            high = weights.at[g, p, turn(outer[p], 1, 4), blocks[block], pl.ds(2, 2)]
            send(("o2r", block, g, p), low, low, rights[outer_axis[p]])
            send(("o2l", block, g, p), high, high, lefts[outer_axis[p]])

    def own_first(part, g):
        for p in range(2):
            ref = weights.at[g, p, outer[p], pair, turn(inner[p], offsets[part], 4)]
            send(("q1r", part, g, p), ref, ref, rights[outer_axis[p]])
            send(("q1l", part, g, p), ref, ref, lefts[outer_axis[p]])

    def own_second(part, g):
        for p in range(2):
            arrived(("q1r", part, g, p), ("q1l", part, g, p))
            at_part = turn(inner[p], offsets[part], 4)
            low = weights.at[g, p, turn(outer[p], -1, 4), pair, at_part, pl.ds(0, PAIR_ROWS)]
            high = weights.at[
                g, p, turn(outer[p], 1, 4), pair, at_part, pl.ds(PAIR_ROWS, PAIR_ROWS)
            ]
            send(("q2r", part, g, p), low, low, rights[outer_axis[p]])
            send(("q2l", part, g, p), high, high, lefts[outer_axis[p]])

    def outer_done(g):
        for p in range(2):
            if g == 0:
                for part in range(4):
                    arrived(("q2r", part, g, p), ("q2l", part, g, p))
            for block in range(1 - g, 4):
                arrived(("o2r", block, g, p), ("o2l", block, g, p))

    def by_x(piece):
        part = pl.ds(piece * 112, 112)
        for xx in range(4):
            acts_x[xx, part] = jnp.concatenate(
                [
                    acts[part, pl.ds(yz * 640, 640)][:, xx * 160 : (xx + 1) * 160]
                    for yz in range(8)
                ],
                axis=1,
            )

    def add(g, p, at_outer, fresh=False):
        tiles = []
        for t in range(2):
            pieces = []
            for i in range(4):
                for zh in range(2):
                    for zl in range(2):
                        part = pl.ds(t * PAIR_ROWS, PAIR_ROWS)
                        pieces.append(weights[g, p, at_outer, zh * 2 + zl, i, part])
            if p == 0:
                pieces = [pieces[i * 4 + zh * 2 + zl] for zh in range(2) for i in range(4) for zl in range(2)]
            tiles.append(jnp.concatenate(pieces, axis=0))
        if p == 0:
            left = acts[:, pl.ds(pl.multiple_of(at_outer * 1280, 1280), 1280)]
        else:
            left = acts_x[at_outer]
        product = jnp.dot(left, jnp.concatenate(tiles, axis=1), preferred_element_type=F32)
        acc[p] = product if fresh else acc[p] + product

    def project_early(g):
        for p in range(2):
            add(g, p, outer[p], True)

        @pl.loop(0, 2)
        def _(k):
            for p in range(2):
                add(g, p, lax.rem(outer[p] + 1 + 2 * k, 4))

    def project(g):
        for p in range(2):
            add(g, p, turn(outer[p], 2, 4))

    def pack(to):
        peaks = []
        for head in range(4):
            p, lanes = head // 2, pl.ds(head % 2 * LANES, LANES)
            for page in range(4):
                part = pl.ds(page * PAGE, PAGE)
                peaks.append(jnp.max(jnp.abs(acc[p, part, lanes]), axis=0, keepdims=True))
        largest = jnp.max(jnp.concatenate(peaks, axis=0), axis=1, keepdims=True)
        scale = ((largest + 1e-06) / 448.0).astype(BF16).astype(F32)
        inverse = 1.0 / scale
        row = lax.broadcasted_iota(jnp.int32, (16, LANES), 0)
        for head in range(4):
            p, lanes = head // 2, pl.ds(head % 2 * LANES, LANES)
            rows = jnp.zeros((16, LANES), F32)
            for page in range(4):
                part = pl.ds(page * PAGE, PAGE)
                k = head * 4 + page
                to[head, part] = (acc[p, part, lanes] * inverse[k : k + 1]).astype(BF16)
                rows = jnp.where(row == page, scale[k : k + 1], rows)
            to[head, pl.ds(CHIP_TOKENS, 16)] = rows.astype(BF16)

    def all_to_all(g):
        for d in range(3):
            send(
                ("a2a", g, d), stage.at[far_chips[d]], pool_ref.at[z_lo], columns[d]
            )
        send(("ahead", 1), stage.at[z_lo, UPPER], relay.at[0, UPPER], ahead)
        send(("behind", 1), stage.at[z_lo, LOWER], relay.at[1, pl.ds(0, 256)], behind)
        for d in (1, 2, 3):
            send(
                ("across", d),
                stage.at[jnp.bitwise_xor(z_lo, d)],
                across_ref.at[z_lo],
                opposite[d],
            )
        own = pltpu.make_async_copy(stage.at[z_lo], pool_ref.at[z_lo], local_sem.at[4])
        own.start()
        return own

    def pass_on():
        arrived(("ahead", 1), ("behind", 1))
        place = jnp.bitwise_xor(z_lo, 2)
        send(("ahead", 2), relay.at[0, UPPER], across_ref.at[place, UPPER], ahead)
        send(("behind", 2), relay.at[1, pl.ds(0, 256)], across_ref.at[place, LOWER], behind)

    line = lax.broadcasted_iota(jnp.int32, (PAGE, LANES), 0)
    def first(page):
        return table_ref[z_lo * 4 + page, dp] * PAGE

    def live(page):
        return first(page) + line < length_ref[dp]

    def angles():
        for copy in small[1:]:
            copy.wait()
        for page in range(4):
            angle = (first(page) + line).astype(F32) * freq_ref[...]
            part = pl.ds(page * PAGE, PAGE)
            turns[0, part], turns[1, part] = trig(angle)
        row = lax.broadcasted_iota(jnp.int32, (FRESH, LANES), 0)
        far_length = length_ref[source_ref[dp]]
        start = jnp.where(jnp.bitwise_and(row, 15) < 8, length_ref[dp], far_length)
        angle = (start + jnp.right_shift(row, 4)).astype(F32) * freq_ref[...]
        part = pl.ds(CHIP_TOKENS, FRESH)
        turns[0, part], turns[1, part] = trig(angle)

    tail = pl.ds(CHIP_TOKENS, FRESH)

    def keep_fresh(kind):
        for head in range(4):
            p, lanes = head // 2, pl.ds(head % 2 * LANES, LANES)

            @pl.when(z_lo == head)
            def _():
                fresh_ref[kind] = acc[p, tail, lanes].astype(BF16)

    def values():
        project(0)
        keep_fresh(1)
        for page in range(4):
            part = pl.ds(page * PAGE, PAGE)
            for head in range(4):
                p, lanes = head // 2, pl.ds(head % 2 * LANES, LANES)
                acc[p, part, lanes] = jnp.where(live(page), acc[p, part, lanes], 0.0)
        pack(stage)

    def keys():
        project(1)
        total = jnp.zeros((ROWS, 1), F32)
        for p in range(2):
            total += jnp.sum(acc[p] * acc[p], axis=1, keepdims=True)
        squares[0] = jnp.broadcast_to(total, (ROWS, LANES))
        send("squares", squares.at[0], squares.at[1], sibling)
        pass_on()
        parts = [pl.ds(page * PAGE, PAGE) for page in range(4)] + [tail]
        for head in range(4):
            p, lanes = head // 2, pl.ds(head % 2 * LANES, LANES)
            gain = gain_ref[pl.ds(head * 2 + core, 1), :]
            for part in parts:
                row = acc[p, part, lanes] * gain
                acc[p, part, lanes] = row * turns[0, part] + pltpu.roll(row, 64, 1) * turns[1, part]
        arrived("squares")
        for page, part in enumerate(parts):
            norm = lax.rsqrt((squares[0, part] + squares[1, part]) * (1.0 / (HEADS * HEAD)) + 1e-06)
            if page < 4:
                norm = jnp.where(live(page), norm, 0.0)
            for head in range(4):
                p, lanes = head // 2, pl.ds(head % 2 * LANES, LANES)
                acc[p, part, lanes] = acc[p, part, lanes] * norm
        keep_fresh(0)
        pack(stage_ref)

    V, K = 0, 1
    assemble(V)
    inner_first(V)
    z_part(1, 0, V)
    own_first(0, V)
    assemble(K)
    z_part(1, 0, K)
    inner_first(K)
    inner_second(V)
    z_part(1, 1, V)
    z_part(1, 2, V)
    own_first(1, V)
    own_first(2, V)
    z_part(2, 0, V)
    own_second(0, V)
    inner_done(V)
    z_part(1, 3, V)
    own_first(3, V)
    z_part(2, 0, K)
    own_second(1, V)
    own_second(2, V)
    z_part(3, 0, V)
    z_part(2, 1, V)
    inner_second(K)
    own_second(3, V)
    z_part(2, 2, V)
    z_part(3, 0, K)
    inner_done(K)
    outer_first(0, K)
    z_part(1, 1, K)
    z_part(3, 1, V)
    z_part(2, 3, V)
    outer_first(1, V)
    angles()
    own_acts.wait()
    for copy in own_decode:
        copy.wait()
    arrived("acts")
    by_x(0)
    z_part(4, 0, V)
    z_part(3, 2, V)
    z_part(4, 0, K)
    z_part(1, 2, K)
    z_part(3, 3, V)
    outer_first(2, V)
    z_part(2, 1, K)
    z_part(4, 1, V)
    z_part(4, 2, V)
    z_part(1, 3, K)
    z_part(2, 2, K)
    z_part(3, 1, K)
    outer_second(1, V)
    by_x(1)
    z_part(4, 3, V)
    by_x(2)
    z_part(2, 3, K)
    z_part(3, 2, K)
    z_part(4, 1, K)
    outer_second(2, V)
    by_x(3)
    z_parts_done(V)
    outer_first(3, V)
    z_part(4, 2, K)
    z_part(3, 3, K)
    z_part(4, 3, K)
    outer_second(0, K)
    outer_second(3, V)
    outer_first(1, K)
    by_x(4)
    project_early(V)
    outer_done(V)
    values()
    own_values = all_to_all(V)
    outer_second(1, K)
    outer_first(2, K)
    z_parts_done(K)
    outer_first(3, K)
    outer_second(2, K)
    outer_second(3, K)
    project_early(K)
    outer_done(K)
    keys()
    own_values.wait()
    for d in range(3):
        arrived(("a2a", V, d))
    for d in (1, 2, 3):
        arrived(("across", d))
    arrived(("ahead", 2), ("behind", 2))
    for copy in copies.values():
        copy.wait_send()


N_COPIES = 7 + 4 * 24 + 2 * 12 + 4 * 12 + 1 + 10


ATTEND_ROWS = GROUP * 3 * 8


def attend(side, q_ref, keys_ref, values_ref, fresh_ref, page_at, length, weight):
    factor = 1.0 / math.sqrt(HEAD)
    steps = 3
    lane = lax.broadcasted_iota(jnp.int32, (1, LANES), 1)
    r = lax.broadcasted_iota(jnp.int32, (ATTEND_ROWS, steps * 8), 0)
    c = lax.broadcasted_iota(jnp.int32, (ATTEND_ROWS, steps * 8), 1)
    visible = (jnp.bitwise_and(r, 7) == jnp.bitwise_and(c, 7)) & (
        jnp.right_shift(lax.rem(r, steps * 8), 3) >= jnp.right_shift(c, 3)
    )
    samples = slice(side * 8, side * 8 + 8)
    query = jnp.concatenate(
        [
            q_ref[:, samples, g * HEAD : (g + 1) * HEAD].astype(F32).reshape(steps * 8, HEAD)
            for g in range(GROUP)
        ],
        axis=0,
    ).astype(BF16)
    new = [
        fresh_ref[kind]
        .astype(F32)
        .reshape(steps, 16, HEAD)[:, samples]
        .reshape(steps * 8, HEAD)
        .astype(BF16)
        for kind in range(2)
    ]
    sums = jnp.zeros((ATTEND_ROWS, LANES), F32)
    for page in range(16):
        chip, part = page // 4, page % 4
        keys = keys_ref[chip, part * PAGE : (part + 1) * PAGE]
        scale = keys_ref[chip, CHIP_TOKENS : CHIP_TOKENS + 16].astype(F32)[part : part + 1]
        raw = lax.dot_general(query, keys, (((1,), (1,)), ((), ())), preferred_element_type=F32)
        live = page_at(page) * PAGE + lane < length
        cached = jnp.where(live, jnp.exp(raw * scale * factor), 0.0)
        weight[:, page * PAGE : (page + 1) * PAGE] = cached
        sums += cached
    fresh_raw = lax.dot_general(
        query, new[0], (((1,), (1,)), ((), ())), preferred_element_type=F32
    )
    fresh = jnp.where(visible, jnp.exp(fresh_raw * factor), 0.0)
    total = jnp.sum(sums, axis=1, keepdims=True) + jnp.sum(fresh, axis=1, keepdims=True)
    result = jnp.dot((fresh / total).astype(BF16), new[1], preferred_element_type=F32)
    for page in range(16):
        chip, part = page // 4, page % 4
        scale = values_ref[chip, CHIP_TOKENS : CHIP_TOKENS + 16].astype(F32)[part : part + 1]
        portion = weight[:, page * PAGE : (page + 1) * PAGE] / total * scale
        result += jnp.dot(
            portion.astype(BF16),
            values_ref[chip, part * PAGE : (part + 1) * PAGE],
            preferred_element_type=F32,
        )
    return [
        result[g * steps * 8 : (g + 1) * steps * 8].reshape(steps, 8, HEAD) for g in range(GROUP)
    ]


def exchange(
    mask, pool_ref, across_ref, stage_ref, far_ref, keys_ref, send_sem, recv_sem, local_sem
):
    dp = lax.axis_index("dp")
    seq = lax.axis_index("seq")
    core = lax.rem(seq, 2)
    z_lo = seq // 2
    partner = jnp.bitwise_xor(dp, mask)
    far_chips = [jnp.bitwise_xor(z_lo, d) for d in (1, 2, 3)]
    columns = [(dp, chip * 2 + core) for chip in far_chips]
    partners = [(partner, jnp.bitwise_xor(z_lo, d) * 2 + core) for d in range(4)]
    plane = mask & ~4
    held = across_ref if mask & 4 else pool_ref
    holder = (jnp.bitwise_xor(dp, plane), seq)

    peers = columns + partners
    if plane and mask & 4:
        peers = peers + [holder]
    barrier = pltpu.get_barrier_semaphore()
    for peer in peers:
        pl.semaphore_signal(barrier, inc=1, device_id=peer, device_id_type=MESH)
    own = pltpu.make_async_copy(stage_ref.at[z_lo], keys_ref.at[z_lo], local_sem.at[0])
    own.start()
    pl.semaphore_wait(barrier, len(peers))

    copies = []

    def send(src, dst, device):
        k = len(copies)
        copy = pltpu.make_async_remote_copy(
            src_ref=src,
            dst_ref=dst,
            send_sem=send_sem.at[k],
            recv_sem=recv_sem.at[k],
            device_id=device,
            device_id_type=MESH,
        )
        copy.start()
        copies.append(copy)

    if plane:
        send(held, far_ref.at[1], holder)
    else:
        local = pltpu.make_async_copy(held, far_ref.at[1], local_sem.at[1])
        local.start()
        local.wait()
    for d in (1, 2, 3):
        send(stage_ref.at[far_chips[d - 1]], keys_ref.at[z_lo], columns[d - 1])
    for d in (3, 2, 1, 0):
        send(stage_ref.at[jnp.bitwise_xor(z_lo, d)], far_ref.at[0, z_lo], partners[d])
    own.wait()
    for copy in copies:
        copy.wait()


def finish(
    q_ref,
    table_ref,
    length_ref,
    source_ref,
    keys_ref,
    values_ref,
    far_ref,
    fresh_ref,
    out_ref,
    fork_ref,
    weight,
):
    dp = lax.axis_index("dp")
    partner = source_ref[dp]
    near = attend(
        0,
        q_ref,
        keys_ref,
        values_ref,
        fresh_ref,
        lambda page: table_ref[page, dp],
        length_ref[dp],
        weight,
    )
    far = attend(
        1,
        q_ref,
        far_ref.at[0],
        far_ref.at[1],
        fresh_ref,
        lambda page: table_ref[page, partner],
        length_ref[partner],
        weight,
    )
    for g in range(GROUP):
        span = slice(g * HEAD, (g + 1) * HEAD)
        out_ref[:, :, span] = jnp.concatenate([near[g], far[g]], axis=1).astype(BF16)
    for kind in range(2):
        for page in range(16):
            chip, part = page // 4, page % 4
            scale = far_ref[kind, chip, CHIP_TOKENS : CHIP_TOKENS + 16].astype(F32)[
                part : part + 1
            ]
            fork_ref[0, kind, page * PAGE : (page + 1) * PAGE] = (
                far_ref[kind, chip, part * PAGE : (part + 1) * PAGE].astype(F32) * scale
            )


def on_device(
    prompt_hidden,
    key_value_weight,
    key_norm_gain,
    page_table,
    lengths,
    source_replica,
    decode_hidden,
    queries,
):
    steps, paired, width = queries.shape
    replicas = lax.axis_size("dp")
    table = page_table.T
    freq = 500000.0 ** (-np.arange(HEAD // 2) * 2.0 / HEAD)
    freq = jnp.asarray(np.concatenate([freq, freq])[None].astype(np.float32))

    vmem = pl.BlockSpec(memory_space=pltpu.VMEM)
    smem = pl.BlockSpec(memory_space=pltpu.SMEM)
    hbm = pl.BlockSpec(memory_space=pl.ANY)
    pinned = pl.BlockSpec(memory_space=pltpu.HBM)
    pool, across, stage, fresh = pl.pallas_call(
        gather_project,
        out_shape=(
            jax.ShapeDtypeStruct((4, SLAB, LANES), BF16),
            jax.ShapeDtypeStruct((4, SLAB, LANES), BF16),
            jax.ShapeDtypeStruct((4, SLAB, LANES), BF16),
            jax.ShapeDtypeStruct((2, FRESH, LANES), BF16),
        ),
        in_specs=[pinned] * 8,
        out_specs=(hbm, hbm, vmem, vmem),
        scratch_shapes=[
            pltpu.VMEM((SHARD, 2 * HEADS * HEAD), BF16),
            pltpu.SMEM((16, 32), jnp.int32),
            pltpu.SMEM((32,), jnp.int32),
            pltpu.SMEM((32,), jnp.int32),
            pltpu.VMEM((1, LANES), F32),
            pltpu.VMEM((HEADS, HEAD), F32),
            pltpu.VMEM((2, 2, PADDED, 4 * LANES), BF16),
            pltpu.VMEM((2, 4, PADDED, 4 * LANES), BF16),
            pltpu.VMEM((ROWS, WIDTH), BF16),
            pltpu.VMEM((4, ROWS, WIDTH // 4), BF16),
            pltpu.VMEM((2, 2, 4, 4, 4, BLOCK, LANES), BF16),
            pltpu.VMEM((2, ROWS, 2 * LANES), F32),
            pltpu.VMEM((4, SLAB, LANES), BF16),
            pltpu.VMEM((2, ROWS, LANES), F32),
            pltpu.VMEM((2, ROWS, LANES), F32),
            pltpu.VMEM((2, 272, LANES), BF16),
            pltpu.SemaphoreType.DMA((N_COPIES,)),
            pltpu.SemaphoreType.DMA((N_COPIES,)),
            pltpu.SemaphoreType.DMA((16,)),
        ],
        compiler_params=pltpu.CompilerParams(
            collective_id=0, has_side_effects=True, vmem_limit_bytes=57 * 1024 * 1024
        ),
    )(
        key_value_weight,
        prompt_hidden,
        decode_hidden,
        table,
        lengths,
        source_replica,
        freq,
        key_norm_gain.reshape(HEADS, HEAD),
    )

    def exchange_by(mask):
        return pl.pallas_call(
            functools.partial(exchange, mask),
            out_shape=(
                jax.ShapeDtypeStruct((2, 4, SLAB, LANES), BF16),
                jax.ShapeDtypeStruct((4, SLAB, LANES), BF16),
            ),
            in_specs=[hbm, hbm, hbm],
            out_specs=(hbm, hbm),
            scratch_shapes=[
                pltpu.SemaphoreType.DMA((8,)),
                pltpu.SemaphoreType.DMA((8,)),
                pltpu.SemaphoreType.DMA((2,)),
            ],
            compiler_params=pltpu.CompilerParams(collective_id=mask, has_side_effects=True),
        )

    far_pool, near_keys = lax.switch(
        source_replica[0] - 1,
        [exchange_by(mask) for mask in range(1, replicas)],
        pool,
        across,
        stage,
    )

    attended, forked = pl.pallas_call(
        finish,
        out_shape=(
            jax.ShapeDtypeStruct((steps, paired, width), BF16),
            jax.ShapeDtypeStruct((1, 2, 2048, LANES), F32),
        ),
        in_specs=[vmem, smem, smem, smem, vmem, vmem, vmem, vmem],
        out_specs=(vmem, vmem),
        scratch_shapes=[pltpu.VMEM((ATTEND_ROWS, 2048), F32)],
        compiler_params=pltpu.CompilerParams(vmem_limit_bytes=32 * 1024 * 1024),
    )(queries, table, lengths, source_replica, near_keys, pool, far_pool, fresh)
    return attended, forked


def solution(mesh):
    return jax.shard_map(
        on_device,
        mesh=mesh,
        in_specs=(
            P("dp", "seq", None),
            P(("dp", "seq"), None),
            P(),
            P(),
            P(),
            P(),
            P(None, "dp", None),
            P(None, "dp", "seq"),
        ),
        out_specs=(P(None, "dp", "seq"), P("dp", None, None, "seq")),
        check_vma=False,
    )
```

```python
import functools
import math

import jax
import jax.numpy as jnp
import numpy as np
from jax import lax
from jax.experimental import pallas as pl
from jax.experimental.pallas import tpu as pltpu
from jax.sharding import PartitionSpec as P

HEADS = 8
HEAD = 128
PAGE = 128
GROUP = 5
MESH = pl.DeviceIdType.MESH
F32 = jnp.float32
BF16 = jnp.bfloat16

WIDTH = 5120
SHARD = 20
PADDED = 32
PAIR_ROWS = 80
BLOCK = 160
TOKENS = 256
CHIP_TOKENS = 512
FRESH = 48
ROWS = CHIP_TOKENS + FRESH
SLAB = CHIP_TOKENS + 16
LANES = 128
UPPER = pl.ds(0, 272)
LOWER = pl.ds(272, 256)


def trig(angle):
    lane = lax.broadcasted_iota(jnp.int32, angle.shape, 1)
    return jnp.cos(angle), jnp.where(lane < HEAD // 2, -jnp.sin(angle), jnp.sin(angle))


def gather_project(
    w_ref,
    prompt_ref,
    decode_ref,
    table_hbm,
    length_hbm,
    source_hbm,
    freq_hbm,
    gain_hbm,
    pool_ref,
    across_ref,
    stage_ref,
    fresh_ref,
    table_ref,
    length_ref,
    source_ref,
    freq_ref,
    gain_ref,
    split,
    raw,
    acts,
    acts_x,
    weights,
    acc,
    stage,
    squares,
    turns,
    relay,
    send_sem,
    recv_sem,
    local_sem,
):
    dp = lax.axis_index("dp")
    seq = lax.axis_index("seq")
    core = lax.rem(seq, 2)
    z_lo = seq // 2
    x = lax.rem(dp, 4)
    z_hi = lax.rem(dp // 4, 2)
    y = dp // 8
    z = z_hi * 4 + z_lo
    pair = z // 2
    odd = lax.rem(z, 2)

    def at(yy, zz, xx, cc):
        return (yy * 8 + (zz // 4) * 4 + xx, lax.rem(zz, 4) * 2 + cc)

    def turn(index, by, size):
        return lax.rem(index + (by + size), size)

    sibling = at(y, z, x, 1 - core)
    inter_z = turn(z, 2 * odd - 1, 8)
    intra_z = z + 1 - 2 * odd
    inter = at(y, inter_z, x, core)
    intra = at(y, intra_z, x, core)
    intra_other = at(y, intra_z, x, 1 - core)
    rights = {"x": at(y, z, turn(x, 1, 4), core), "y": at(turn(y, 1, 4), z, x, core)}
    lefts = {"x": at(y, z, turn(x, -1, 4), core), "y": at(turn(y, -1, 4), z, x, core)}
    far_chips = [jnp.bitwise_xor(z_lo, d) for d in (1, 2, 3)]
    columns = [(dp, chip * 2 + core) for chip in far_chips]
    opposite = [
        (jnp.bitwise_xor(dp, 4), jnp.bitwise_xor(z_lo, d) * 2 + core) for d in range(4)
    ]

    ahead = at(y, turn(z, 2, 8), x, core)
    behind = at(y, turn(z, -2, 8), x, core)

    peers = opposite[1:] + [
        ahead,
        behind,
        sibling,
        inter,
        intra,
        intra_other,
        rights["x"],
        lefts["x"],
        rights["y"],
        lefts["y"],
        columns[1],
        columns[2],
    ]
    barrier = pltpu.get_barrier_semaphore()
    for peer in peers:
        pl.semaphore_signal(barrier, inc=1, device_id=peer, device_id_type=MESH)

    small = [
        pltpu.make_async_copy(src, dst, local_sem.at[8 + k])
        for k, (src, dst) in enumerate(
            [
                (table_hbm, table_ref),
                (length_hbm, length_ref),
                (source_hbm, source_ref),
                (freq_hbm, freq_ref),
                (gain_hbm, gain_ref),
            ]
        )
    ]
    for copy in small:
        copy.start()
    own_acts = pltpu.make_async_copy(
        prompt_ref.at[0],
        acts.at[pl.ds(pl.multiple_of(core * TOKENS, TOKENS), TOKENS)],
        local_sem.at[0],
    )
    own_acts.start()
    own_decode = [
        pltpu.make_async_copy(
            decode_ref.at[step], acts.at[pl.ds(CHIP_TOKENS + step * 16, 16)], local_sem.at[1 + step]
        )
        for step in range(3)
    ]
    for copy in own_decode:
        copy.start()

    for g in range(2):
        for c in range(2):
            tiles = [
                w_ref[:, pl.ds((1 - g) * HEADS * HEAD + (2 * i + c) * HEAD, HEAD)] for i in range(4)
            ]
            split[g, c] = jnp.concatenate(tiles, axis=1)
        raw[g, odd * 2 + core] = split[g, core]
    pl.semaphore_wait(barrier, len(peers))

    number = [0]
    copies = {}

    def send(key, src, dst, device):
        k = number[0]
        number[0] += 1
        copy = pltpu.make_async_remote_copy(
            src_ref=src,
            dst_ref=dst,
            send_sem=send_sem.at[k],
            recv_sem=recv_sem.at[k],
            device_id=device,
            device_id_type=MESH,
        )
        copy.start()
        copies[key] = copy

    def arrived(*keys):
        for key in keys:
            copies[key].wait_recv()

    slot = odd * 2 + core
    for g in range(2):
        send(("w_intra", g), split.at[g, core], raw.at[g, slot], intra)
        send(("w_other", g), split.at[g, 1 - core], raw.at[g, slot], intra_other)
        send(("w_sibling", g), split.at[g, 1 - core], raw.at[g, slot], sibling)

    here = pl.ds(pl.multiple_of(core * TOKENS, TOKENS), TOKENS)
    send("acts", prompt_ref.at[0], acts.at[here], sibling)

    row = lax.broadcasted_iota(jnp.int32, (PAIR_ROWS, 4 * PADDED), 0)
    col = lax.broadcasted_iota(jnp.int32, (PAIR_ROWS, 4 * PADDED), 1)
    inside = jnp.bitwise_and(col, PADDED - 1)
    source = jnp.right_shift(col, 5)
    pick = jnp.where((row == source * SHARD + inside) & (inside < SHARD), 1.0, 0.0).astype(BF16)

    outer = (y, x)
    inner = (x, y)
    inner_axis = ("x", "y")
    outer_axis = ("y", "x")

    def assemble(g):
        arrived(("w_intra", g), ("w_other", g), ("w_sibling", g))
        rows = jnp.dot(
            pick, raw[g].reshape(4 * PADDED, 4 * LANES), preferred_element_type=F32
        ).astype(BF16)
        for p in range(2):
            for t in range(2):
                tile = p * 2 + t
                weights[g, p, outer[p], pair, inner[p], pl.ds(t * PAIR_ROWS, PAIR_ROWS)] = rows[
                    :, tile * LANES : (tile + 1) * LANES
                ]

    offsets = (0, -1, 1, 2)
    sign = 2 * odd - 1
    blocks = [pair, turn(pair, sign, 4), turn(pair, -sign, 4), turn(pair, 2, 4)]

    def inner_first(g):
        for p in range(2):
            ref = weights.at[g, p, outer[p], pair, inner[p]]
            send(("i1r", g, p), ref, ref, rights[inner_axis[p]])
            send(("i1l", g, p), ref, ref, lefts[inner_axis[p]])

    def inner_second(g):
        for p in range(2):
            arrived(("i1r", g, p), ("i1l", g, p))
            ref = weights.at[g, p, outer[p], pair]
            low = ref.at[turn(inner[p], -1, 4), pl.ds(0, PAIR_ROWS)]
            high = ref.at[turn(inner[p], 1, 4), pl.ds(PAIR_ROWS, PAIR_ROWS)]
            send(("i2r", g, p), low, low, rights[inner_axis[p]])
            send(("i2l", g, p), high, high, lefts[inner_axis[p]])

    def inner_done(g):
        for p in range(2):
            arrived(("i2r", g, p), ("i2l", g, p))

    def z_step(step, g):
        half = (1 - odd) if step == 3 else odd
        for p in range(2):
            if step >= 2:
                arrived(("z", step - 1, g, p))
            ref = weights.at[g, p, outer[p], blocks[step - 1]]
            if step >= 3:
                ref = ref.at[pl.ds(half * 2, 2)]
            send(("z", step, g, p), ref, ref, inter if step % 2 else intra)

    def z_part(step, part, g):
        half = (1 - odd) if step == 3 else odd
        for p in range(2):
            at_part = turn(inner[p], offsets[part], 4)
            if step >= 2:
                arrived(("zp", step - 1, part, g, p))
            ref = weights.at[g, p, outer[p], blocks[step - 1], at_part]
            if step >= 3:
                ref = ref.at[pl.ds(pl.multiple_of(half * PAIR_ROWS, 16), PAIR_ROWS)]
            send(("zp", step, part, g, p), ref, ref, inter if step % 2 else intra)

    def z_parts_done(g):
        for part in range(4):
            for p in range(2):
                arrived(("zp", 4, part, g, p))

    def z_done(g):
        for p in range(2):
            arrived(("z", 4, g, p))

    def outer_first(block, g):
        for p in range(2):
            ref = weights.at[g, p, outer[p], blocks[block]]
            send(("o1r", block, g, p), ref, ref, rights[outer_axis[p]])
            send(("o1l", block, g, p), ref, ref, lefts[outer_axis[p]])

    def outer_second(block, g):
        for p in range(2):
            arrived(("o1r", block, g, p), ("o1l", block, g, p))
            low = weights.at[g, p, turn(outer[p], -1, 4), blocks[block], pl.ds(0, 2)]
            high = weights.at[g, p, turn(outer[p], 1, 4), blocks[block], pl.ds(2, 2)]
            send(("o2r", block, g, p), low, low, rights[outer_axis[p]])
            send(("o2l", block, g, p), high, high, lefts[outer_axis[p]])

    def own_first(part, g):
        for p in range(2):
            ref = weights.at[g, p, outer[p], pair, turn(inner[p], offsets[part], 4)]
            send(("q1r", part, g, p), ref, ref, rights[outer_axis[p]])
            send(("q1l", part, g, p), ref, ref, lefts[outer_axis[p]])

    def own_second(part, g):
        for p in range(2):
            arrived(("q1r", part, g, p), ("q1l", part, g, p))
            at_part = turn(inner[p], offsets[part], 4)
            low = weights.at[g, p, turn(outer[p], -1, 4), pair, at_part, pl.ds(0, PAIR_ROWS)]
            high = weights.at[
                g, p, turn(outer[p], 1, 4), pair, at_part, pl.ds(PAIR_ROWS, PAIR_ROWS)
            ]
            send(("q2r", part, g, p), low, low, rights[outer_axis[p]])
            send(("q2l", part, g, p), high, high, lefts[outer_axis[p]])

    def outer_done(g):
        for p in range(2):
            if g == 0:
                for part in range(4):
                    arrived(("q2r", part, g, p), ("q2l", part, g, p))
            for block in range(1 - g, 4):
                arrived(("o2r", block, g, p), ("o2l", block, g, p))

    def by_x(piece):
        part = pl.ds(piece * 112, 112)
        for xx in range(4):
            acts_x[xx, part] = jnp.concatenate(
                [
                    acts[part, pl.ds(yz * 640, 640)][:, xx * 160 : (xx + 1) * 160]
                    for yz in range(8)
                ],
                axis=1,
            )

    def add(g, p, at_outer, fresh=False):
        tiles = []
        for t in range(2):
            pieces = []
            for i in range(4):
                for zh in range(2):
                    for zl in range(2):
                        part = pl.ds(t * PAIR_ROWS, PAIR_ROWS)
                        pieces.append(weights[g, p, at_outer, zh * 2 + zl, i, part])
            if p == 0:
                pieces = [pieces[i * 4 + zh * 2 + zl] for zh in range(2) for i in range(4) for zl in range(2)]
            tiles.append(jnp.concatenate(pieces, axis=0))
        if p == 0:
            left = acts[:, pl.ds(pl.multiple_of(at_outer * 1280, 1280), 1280)]
        else:
            left = acts_x[at_outer]
        product = jnp.dot(left, jnp.concatenate(tiles, axis=1), preferred_element_type=F32)
        acc[p] = product if fresh else acc[p] + product

    def project_early(g):
        for p in range(2):
            add(g, p, outer[p], True)

        @pl.loop(0, 2)
        def _(k):
            for p in range(2):
                add(g, p, lax.rem(outer[p] + 1 + 2 * k, 4))

    def project(g):
        for p in range(2):
            add(g, p, turn(outer[p], 2, 4))

    def pack(to):
        peaks = []
        for head in range(4):
            p, lanes = head // 2, pl.ds(head % 2 * LANES, LANES)
            for page in range(4):
                part = pl.ds(page * PAGE, PAGE)
                peaks.append(jnp.max(jnp.abs(acc[p, part, lanes]), axis=0, keepdims=True))
        largest = jnp.max(jnp.concatenate(peaks, axis=0), axis=1, keepdims=True)
        scale = ((largest + 1e-06) / 448.0).astype(BF16).astype(F32)
        inverse = 1.0 / scale
        row = lax.broadcasted_iota(jnp.int32, (16, LANES), 0)
        for head in range(4):
            p, lanes = head // 2, pl.ds(head % 2 * LANES, LANES)
            rows = jnp.zeros((16, LANES), F32)
            for page in range(4):
                part = pl.ds(page * PAGE, PAGE)
                k = head * 4 + page
                to[head, part] = (acc[p, part, lanes] * inverse[k : k + 1]).astype(BF16)
                rows = jnp.where(row == page, scale[k : k + 1], rows)
            to[head, pl.ds(CHIP_TOKENS, 16)] = rows.astype(BF16)

    def all_to_all(g):
        for d in range(3):
            send(
                ("a2a", g, d), stage.at[far_chips[d]], pool_ref.at[z_lo], columns[d]
            )
        send(("ahead", 1), stage.at[z_lo, UPPER], relay.at[0, UPPER], ahead)
        send(("behind", 1), stage.at[z_lo, LOWER], relay.at[1, pl.ds(0, 256)], behind)
        for d in (1, 2, 3):
            send(
                ("across", d),
                stage.at[jnp.bitwise_xor(z_lo, d)],
                across_ref.at[z_lo],
                opposite[d],
            )
        own = pltpu.make_async_copy(stage.at[z_lo], pool_ref.at[z_lo], local_sem.at[4])
        own.start()
        return own

    def pass_on():
        arrived(("ahead", 1), ("behind", 1))
        place = jnp.bitwise_xor(z_lo, 2)
        send(("ahead", 2), relay.at[0, UPPER], across_ref.at[place, UPPER], ahead)
        send(("behind", 2), relay.at[1, pl.ds(0, 256)], across_ref.at[place, LOWER], behind)

    line = lax.broadcasted_iota(jnp.int32, (PAGE, LANES), 0)
    def first(page):
        return table_ref[z_lo * 4 + page, dp] * PAGE

    def live(page):
        return first(page) + line < length_ref[dp]

    def angles():
        for copy in small:
            copy.wait()
        for page in range(4):
            angle = (first(page) + line).astype(F32) * freq_ref[...]
            part = pl.ds(page * PAGE, PAGE)
            turns[0, part], turns[1, part] = trig(angle)
        row = lax.broadcasted_iota(jnp.int32, (FRESH, LANES), 0)
        far_length = length_ref[source_ref[dp]]
        start = jnp.where(jnp.bitwise_and(row, 15) < 8, length_ref[dp], far_length)
        angle = (start + jnp.right_shift(row, 4)).astype(F32) * freq_ref[...]
        part = pl.ds(CHIP_TOKENS, FRESH)
        turns[0, part], turns[1, part] = trig(angle)

    tail = pl.ds(CHIP_TOKENS, FRESH)

    def keep_fresh(kind):
        for head in range(4):
            p, lanes = head // 2, pl.ds(head % 2 * LANES, LANES)

            @pl.when(z_lo == head)
            def _():
                fresh_ref[kind] = acc[p, tail, lanes].astype(BF16)

    def values():
        project(0)
        keep_fresh(1)
        for page in range(4):
            part = pl.ds(page * PAGE, PAGE)
            for head in range(4):
                p, lanes = head // 2, pl.ds(head % 2 * LANES, LANES)
                acc[p, part, lanes] = jnp.where(live(page), acc[p, part, lanes], 0.0)
        pack(stage)

    def keys():
        project(1)
        total = jnp.zeros((ROWS, 1), F32)
        for p in range(2):
            total += jnp.sum(acc[p] * acc[p], axis=1, keepdims=True)
        squares[0] = jnp.broadcast_to(total, (ROWS, LANES))
        send("squares", squares.at[0], squares.at[1], sibling)
        pass_on()
        parts = [pl.ds(page * PAGE, PAGE) for page in range(4)] + [tail]
        for head in range(4):
            p, lanes = head // 2, pl.ds(head % 2 * LANES, LANES)
            gain = gain_ref[pl.ds(head * 2 + core, 1), :]
            for part in parts:
                row = acc[p, part, lanes] * gain
                acc[p, part, lanes] = row * turns[0, part] + pltpu.roll(row, 64, 1) * turns[1, part]
        arrived("squares")
        for page, part in enumerate(parts):
            norm = lax.rsqrt((squares[0, part] + squares[1, part]) * (1.0 / (HEADS * HEAD)) + 1e-06)
            if page < 4:
                norm = jnp.where(live(page), norm, 0.0)
            for head in range(4):
                p, lanes = head // 2, pl.ds(head % 2 * LANES, LANES)
                acc[p, part, lanes] = acc[p, part, lanes] * norm
        keep_fresh(0)
        pack(stage_ref)

    V, K = 0, 1
    assemble(V)
    inner_first(V)
    z_part(1, 0, V)
    own_first(0, V)
    assemble(K)
    z_part(1, 0, K)
    inner_first(K)
    inner_second(V)
    z_part(1, 1, V)
    z_part(1, 2, V)
    own_first(1, V)
    own_first(2, V)
    z_part(2, 0, V)
    own_second(0, V)
    inner_done(V)
    z_part(1, 3, V)
    own_first(3, V)
    z_part(2, 0, K)
    own_second(1, V)
    own_second(2, V)
    z_part(3, 0, V)
    z_part(2, 1, V)
    inner_second(K)
    own_second(3, V)
    z_part(2, 2, V)
    z_part(3, 0, K)
    inner_done(K)
    outer_first(0, K)
    z_part(1, 1, K)
    z_part(3, 1, V)
    z_part(2, 3, V)
    outer_first(1, V)
    angles()
    own_acts.wait()
    for copy in own_decode:
        copy.wait()
    arrived("acts")
    by_x(0)
    z_part(4, 0, V)
    z_part(3, 2, V)
    z_part(4, 0, K)
    z_part(1, 2, K)
    z_part(3, 3, V)
    outer_first(2, V)
    z_part(2, 1, K)
    z_part(4, 1, V)
    z_part(4, 2, V)
    z_part(1, 3, K)
    z_part(2, 2, K)
    z_part(3, 1, K)
    outer_second(1, V)
    by_x(1)
    z_part(4, 3, V)
    by_x(2)
    z_part(2, 3, K)
    z_part(3, 2, K)
    z_part(4, 1, K)
    outer_second(2, V)
    by_x(3)
    z_parts_done(V)
    outer_first(3, V)
    z_part(4, 2, K)
    z_part(3, 3, K)
    z_part(4, 3, K)
    outer_second(0, K)
    outer_second(3, V)
    outer_first(1, K)
    by_x(4)
    project_early(V)
    outer_done(V)
    values()
    own_values = all_to_all(V)
    outer_second(1, K)
    outer_first(2, K)
    z_parts_done(K)
    outer_first(3, K)
    outer_second(2, K)
    outer_second(3, K)
    project_early(K)
    outer_done(K)
    keys()
    own_values.wait()
    for d in range(3):
        arrived(("a2a", V, d))
    for d in (1, 2, 3):
        arrived(("across", d))
    arrived(("ahead", 2), ("behind", 2))
    for copy in copies.values():
        copy.wait_send()


N_COPIES = 7 + 4 * 24 + 2 * 12 + 4 * 12 + 1 + 10


ATTEND_ROWS = GROUP * 3 * 8


def attend(side, q_ref, keys_ref, values_ref, fresh_ref, page_at, length, weight):
    factor = 1.0 / math.sqrt(HEAD)
    steps = 3
    lane = lax.broadcasted_iota(jnp.int32, (1, LANES), 1)
    r = lax.broadcasted_iota(jnp.int32, (ATTEND_ROWS, steps * 8), 0)
    c = lax.broadcasted_iota(jnp.int32, (ATTEND_ROWS, steps * 8), 1)
    visible = (jnp.bitwise_and(r, 7) == jnp.bitwise_and(c, 7)) & (
        jnp.right_shift(lax.rem(r, steps * 8), 3) >= jnp.right_shift(c, 3)
    )
    samples = slice(side * 8, side * 8 + 8)
    query = jnp.concatenate(
        [
            q_ref[:, samples, g * HEAD : (g + 1) * HEAD].astype(F32).reshape(steps * 8, HEAD)
            for g in range(GROUP)
        ],
        axis=0,
    ).astype(BF16)
    new = [
        fresh_ref[kind]
        .astype(F32)
        .reshape(steps, 16, HEAD)[:, samples]
        .reshape(steps * 8, HEAD)
        .astype(BF16)
        for kind in range(2)
    ]
    sums = jnp.zeros((ATTEND_ROWS, LANES), F32)
    for page in range(16):
        chip, part = page // 4, page % 4
        keys = keys_ref[chip, part * PAGE : (part + 1) * PAGE]
        scale = keys_ref[chip, CHIP_TOKENS : CHIP_TOKENS + 16].astype(F32)[part : part + 1]
        raw = lax.dot_general(query, keys, (((1,), (1,)), ((), ())), preferred_element_type=F32)
        live = page_at(page) * PAGE + lane < length
        cached = jnp.where(live, jnp.exp(raw * scale * factor), 0.0)
        weight[:, page * PAGE : (page + 1) * PAGE] = cached
        sums += cached
    fresh_raw = lax.dot_general(
        query, new[0], (((1,), (1,)), ((), ())), preferred_element_type=F32
    )
    fresh = jnp.where(visible, jnp.exp(fresh_raw * factor), 0.0)
    total = jnp.sum(sums, axis=1, keepdims=True) + jnp.sum(fresh, axis=1, keepdims=True)
    result = jnp.dot((fresh / total).astype(BF16), new[1], preferred_element_type=F32)
    for page in range(16):
        chip, part = page // 4, page % 4
        scale = values_ref[chip, CHIP_TOKENS : CHIP_TOKENS + 16].astype(F32)[part : part + 1]
        portion = weight[:, page * PAGE : (page + 1) * PAGE] / total * scale
        result += jnp.dot(
            portion.astype(BF16),
            values_ref[chip, part * PAGE : (part + 1) * PAGE],
            preferred_element_type=F32,
        )
    return [
        result[g * steps * 8 : (g + 1) * steps * 8].reshape(steps, 8, HEAD) for g in range(GROUP)
    ]


def exchange(
    mask, pool_ref, across_ref, stage_ref, far_ref, keys_ref, send_sem, recv_sem, local_sem
):
    dp = lax.axis_index("dp")
    seq = lax.axis_index("seq")
    core = lax.rem(seq, 2)
    z_lo = seq // 2
    partner = jnp.bitwise_xor(dp, mask)
    far_chips = [jnp.bitwise_xor(z_lo, d) for d in (1, 2, 3)]
    columns = [(dp, chip * 2 + core) for chip in far_chips]
    partners = [(partner, jnp.bitwise_xor(z_lo, d) * 2 + core) for d in range(4)]
    plane = mask & ~4
    held = across_ref if mask & 4 else pool_ref
    holder = (jnp.bitwise_xor(dp, plane), seq)

    peers = columns + partners
    if plane and mask & 4:
        peers = peers + [holder]
    barrier = pltpu.get_barrier_semaphore()
    for peer in peers:
        pl.semaphore_signal(barrier, inc=1, device_id=peer, device_id_type=MESH)
    own = pltpu.make_async_copy(stage_ref.at[z_lo], keys_ref.at[z_lo], local_sem.at[0])
    own.start()
    pl.semaphore_wait(barrier, len(peers))

    copies = []

    def send(src, dst, device):
        k = len(copies)
        copy = pltpu.make_async_remote_copy(
            src_ref=src,
            dst_ref=dst,
            send_sem=send_sem.at[k],
            recv_sem=recv_sem.at[k],
            device_id=device,
            device_id_type=MESH,
        )
        copy.start()
        copies.append(copy)

    if plane:
        send(held, far_ref.at[1], holder)
    else:
        local = pltpu.make_async_copy(held, far_ref.at[1], local_sem.at[1])
        local.start()
        local.wait()
    for d in (1, 2, 3):
        send(stage_ref.at[far_chips[d - 1]], keys_ref.at[z_lo], columns[d - 1])
    for d in (3, 2, 1, 0):
        send(stage_ref.at[jnp.bitwise_xor(z_lo, d)], far_ref.at[0, z_lo], partners[d])
    own.wait()
    for copy in copies:
        copy.wait()


def finish(
    q_ref,
    table_ref,
    length_ref,
    source_ref,
    keys_ref,
    values_ref,
    far_ref,
    fresh_ref,
    out_ref,
    fork_ref,
    weight,
):
    dp = lax.axis_index("dp")
    partner = source_ref[dp]
    near = attend(
        0,
        q_ref,
        keys_ref,
        values_ref,
        fresh_ref,
        lambda page: table_ref[page, dp],
        length_ref[dp],
        weight,
    )
    far = attend(
        1,
        q_ref,
        far_ref.at[0],
        far_ref.at[1],
        fresh_ref,
        lambda page: table_ref[page, partner],
        length_ref[partner],
        weight,
    )
    for g in range(GROUP):
        span = slice(g * HEAD, (g + 1) * HEAD)
        out_ref[:, :, span] = jnp.concatenate([near[g], far[g]], axis=1).astype(BF16)
    for kind in range(2):
        for page in range(16):
            chip, part = page // 4, page % 4
            scale = far_ref[kind, chip, CHIP_TOKENS : CHIP_TOKENS + 16].astype(F32)[
                part : part + 1
            ]
            fork_ref[0, kind, page * PAGE : (page + 1) * PAGE] = (
                far_ref[kind, chip, part * PAGE : (part + 1) * PAGE].astype(F32) * scale
            )


def on_device(
    prompt_hidden,
    key_value_weight,
    key_norm_gain,
    page_table,
    lengths,
    source_replica,
    decode_hidden,
    queries,
):
    steps, paired, width = queries.shape
    replicas = lax.axis_size("dp")
    table = page_table.T
    freq = 500000.0 ** (-np.arange(HEAD // 2) * 2.0 / HEAD)
    freq = jnp.asarray(np.concatenate([freq, freq])[None].astype(np.float32))

    vmem = pl.BlockSpec(memory_space=pltpu.VMEM)
    smem = pl.BlockSpec(memory_space=pltpu.SMEM)
    hbm = pl.BlockSpec(memory_space=pl.ANY)
    pinned = pl.BlockSpec(memory_space=pltpu.HBM)
    pool, across, stage, fresh = pl.pallas_call(
        gather_project,
        out_shape=(
            jax.ShapeDtypeStruct((4, SLAB, LANES), BF16),
            jax.ShapeDtypeStruct((4, SLAB, LANES), BF16),
            jax.ShapeDtypeStruct((4, SLAB, LANES), BF16),
            jax.ShapeDtypeStruct((2, FRESH, LANES), BF16),
        ),
        in_specs=[vmem] + [pinned] * 7,
        out_specs=(hbm, hbm, vmem, vmem),
        scratch_shapes=[
            pltpu.SMEM((16, 32), jnp.int32),
            pltpu.SMEM((32,), jnp.int32),
            pltpu.SMEM((32,), jnp.int32),
            pltpu.VMEM((1, LANES), F32),
            pltpu.VMEM((HEADS, HEAD), F32),
            pltpu.VMEM((2, 2, PADDED, 4 * LANES), BF16),
            pltpu.VMEM((2, 4, PADDED, 4 * LANES), BF16),
            pltpu.VMEM((ROWS, WIDTH), BF16),
            pltpu.VMEM((4, ROWS, WIDTH // 4), BF16),
            pltpu.VMEM((2, 2, 4, 4, 4, BLOCK, LANES), BF16),
            pltpu.VMEM((2, ROWS, 2 * LANES), F32),
            pltpu.VMEM((4, SLAB, LANES), BF16),
            pltpu.VMEM((2, ROWS, LANES), F32),
            pltpu.VMEM((2, ROWS, LANES), F32),
            pltpu.VMEM((2, 272, LANES), BF16),
            pltpu.SemaphoreType.DMA((N_COPIES,)),
            pltpu.SemaphoreType.DMA((N_COPIES,)),
            pltpu.SemaphoreType.DMA((16,)),
        ],
        compiler_params=pltpu.CompilerParams(
            collective_id=0, has_side_effects=True, vmem_limit_bytes=57 * 1024 * 1024
        ),
    )(
        jnp.pad(key_value_weight, ((0, PADDED - SHARD), (0, 0))),
        prompt_hidden,
        decode_hidden,
        table,
        lengths,
        source_replica,
        freq,
        key_norm_gain.reshape(HEADS, HEAD),
    )

    def exchange_by(mask):
        return pl.pallas_call(
            functools.partial(exchange, mask),
            out_shape=(
                jax.ShapeDtypeStruct((2, 4, SLAB, LANES), BF16),
                jax.ShapeDtypeStruct((4, SLAB, LANES), BF16),
            ),
            in_specs=[hbm, hbm, hbm],
            out_specs=(hbm, hbm),
            scratch_shapes=[
                pltpu.SemaphoreType.DMA((8,)),
                pltpu.SemaphoreType.DMA((8,)),
                pltpu.SemaphoreType.DMA((2,)),
            ],
            compiler_params=pltpu.CompilerParams(collective_id=mask, has_side_effects=True),
        )

    far_pool, near_keys = lax.switch(
        source_replica[0] - 1,
        [exchange_by(mask) for mask in range(1, replicas)],
        pool,
        across,
        stage,
    )

    attended, forked = pl.pallas_call(
        finish,
        out_shape=(
            jax.ShapeDtypeStruct((steps, paired, width), BF16),
            jax.ShapeDtypeStruct((1, 2, 2048, LANES), F32),
        ),
        in_specs=[vmem, smem, smem, smem, vmem, vmem, vmem, vmem],
        out_specs=(vmem, vmem),
        scratch_shapes=[pltpu.VMEM((ATTEND_ROWS, 2048), F32)],
        compiler_params=pltpu.CompilerParams(vmem_limit_bytes=32 * 1024 * 1024),
    )(queries, table, lengths, source_replica, near_keys, pool, far_pool, fresh)
    return attended, forked


def solution(mesh):
    return jax.shard_map(
        on_device,
        mesh=mesh,
        in_specs=(
            P("dp", "seq", None),
            P(("dp", "seq"), None),
            P(),
            P(),
            P(),
            P(),
            P(None, "dp", None),
            P(None, "dp", "seq"),
        ),
        out_specs=(P(None, "dp", "seq"), P("dp", None, None, "seq")),
        check_vma=False,
    )
```
